128 devices in a mesh: dp: 16 (over y, x_hi, core), tensor: 8 (over z, x_lo).
Axes of the slice: x: 4 (x_hi: 2, x_lo: 2; x = x_hi * 2 + x_lo), y: 4, z: 4, core: 2. Of those that a mesh axis runs over, the one named last changes fastest.
Arguments:
- q_latent: bfloat16 [16384, 1536], P(('dp', 'tensor')), may hold values from -6 to 6
- kv_compressed: bfloat16 [16384, 576], P(('dp', 'tensor')), may hold values from -110 to 110
- q_gain: float32 [1536], replicated, may hold values from 0.1 to 1.9
- kv_gain: float32 [512], replicated, may hold values from 0.1 to 1.9
- wq_b: bfloat16 [1536, 12288], P('dp', 'tensor'), may hold values from -0.15625 to 0.15625
- wkv_b: bfloat16 [512, 16384], P('dp', 'tensor'), may hold values from -0.25 to 0.25
- wo: bfloat16 [8192, 7168], P('tensor', 'dp'), may hold values from -0.0625 to 0.0625
Outputs:
- mixed: bfloat16 [16384, 7168], P(('dp', 'tensor'))
The draws below stay inside these ranges and needn't reach their ends.
All inputs are finite; a program needn't handle non-finite values.
Results may differ from the reference program's by a relative error of at most 0.018.
The reference program's roundings to bfloat16 on the way (of `q_norm`, `kv_norm`, `k_rot`, `kv_full`, `probs`, `attn` and `partials`) count: a program that leaves them out, or rounds other values in their place, can miss the bound.
Values may be sent and summed in bfloat16 or wider, within the bound.
No kernel may reach another device: no remote copies, remote signals or barrier semaphores. Data moves between devices by JAX's collectives and lax.ppermute only.
A program may use at most 128 MiB of HBM per device.

```python
import jax
import jax.numpy as jnp
from jax import lax

D = 7168
HEADS = 64
NOPE = 128
R = 64
V = 128
QL = 1536
KL = 512
SEQ = 1024
TOKENS = 16384
N_DP = 16
N_TENSOR = 8


def draw_kv_compressed(key, part):
    key = jax.random.fold_in(key, 7)
    key_base = jax.random.fold_in(key, 0)
    base_draw = jnp.clip(jax.random.normal(key_base, (TOKENS, KL + R), jnp.float32), -6.0, 6.0)
    return base_draw.astype(jnp.bfloat16)


def level_of(rng, shape, pieces, least, largest):
    level, own = 1.0, jax.random.fold_in(rng, 6)
    for axis_at, blocks in pieces:
        steps = jnp.exp(jax.random.uniform(jax.random.fold_in(own, axis_at), (blocks,), jnp.float32, least / len(pieces), largest / len(pieces)))
        level = level * jnp.repeat(steps, shape[axis_at] // blocks).reshape([-1 if axis == axis_at else 1 for axis in range(len(shape))])
    return level


def scatter_about(rng, shape, scale, reach, pieces=(), kind=jnp.bfloat16):
    factor_of = level_of(rng, shape, pieces, -0.22, 0.18) if pieces else 1.0
    drawn = jax.random.normal(rng, shape, jnp.float32) * scale * factor_of
    return jnp.minimum(jnp.maximum(drawn, -reach), reach).astype(kind)


def setup_inputs(seed: int = 0) -> dict:
    splits = jax.random.split(jax.random.key(seed), 8)
    q_latent = scatter_about(splits[0], (TOKENS, QL), 1.0, 6.0, ((0, 128),))
    kv_compressed = draw_kv_compressed(jax.random.fold_in(splits[7], 71), 0)
    q_gain = jnp.clip(1.0 + 0.18 * jax.random.normal(splits[2], (QL,), jnp.float32), 0.1, 1.9)
    kv_gain = jnp.clip(1.0 + 0.18 * jax.random.normal(splits[3], (KL,), jnp.float32), 0.1, 1.9)
    wq_b = scatter_about(splits[4], (QL, HEADS * (NOPE + R)), QL ** -0.5, 0.15625, ((0, 16), (1, 8)))
    wkv_b = scatter_about(splits[5], (KL, HEADS * (NOPE + V)), KL ** -0.5, 0.25, ((0, 16), (1, 8)))
    wo = scatter_about(splits[6], (HEADS * V, D), (HEADS * V) ** -0.5, 0.0625, ((0, 8), (1, 16)))
    return dict(q_latent=q_latent, kv_compressed=kv_compressed, q_gain=q_gain, kv_gain=kv_gain, wq_b=wq_b, wkv_b=wkv_b, wo=wo)


epsilon = 1e-06

def rms_scale(values_in, gain):
    widened = values_in.astype(jnp.float32)
    return widened * lax.rsqrt(lax.optimization_barrier(jnp.mean(widened * widened, axis=-1, keepdims=True)) + epsilon) * gain

def rotary_tables(positions, width):
    half_width = width // 2
    frequency = 10000.0 ** (-jnp.arange(half_width, dtype=jnp.float32) / half_width)
    angles = positions[:, None] * frequency[None, :]
    return (jnp.cos(angles), jnp.sin(angles))

def rotate(vectors, cosine, sine):
    half_width = vectors.shape[-1] // 2
    first_half = vectors[..., :half_width]
    second_half = vectors[..., half_width:]
    return jnp.concatenate([first_half * cosine - second_half * sine, second_half * cosine + first_half * sine], axis=-1)

def one_sequence(q_rows, kv_rows, q_gain, kv_gain, wq_b, wkv_b, wo):
    length = q_rows.shape[0]
    positions = jnp.arange(length, dtype=jnp.float32)
    cosine, sine = rotary_tables(positions, R)
    q_norm = rms_scale(q_rows, q_gain).astype(jnp.bfloat16)
    kv_norm = rms_scale(kv_rows[:, :KL], kv_gain).astype(jnp.bfloat16)
    k_rot = rotate(kv_rows[:, KL:].astype(jnp.float32), cosine, sine).astype(jnp.bfloat16)
    q_full = jnp.dot(q_norm, wq_b, preferred_element_type=jnp.float32).reshape(length, HEADS, NOPE + R)
    q_nope = q_full[..., :NOPE].astype(jnp.bfloat16)
    q_rot = rotate(q_full[..., NOPE:], cosine[:, None, :], sine[:, None, :]).astype(jnp.bfloat16)
    kv_full = jnp.dot(kv_norm, wkv_b, preferred_element_type=jnp.float32).astype(jnp.bfloat16)
    kv_full = kv_full.reshape(length, HEADS, NOPE + V)
    k_nope = kv_full[..., :NOPE]
    values = kv_full[..., NOPE:]
    causal = positions[:, None] >= positions[None, :]
    factor = 1.0 / (NOPE + R) ** 0.5

    def one_head(operands):
        query_nope, query_rot, key_nope, head_values = operands
        scores = jnp.dot(query_nope, key_nope.T, preferred_element_type=jnp.float32)
        scores = (scores + jnp.dot(query_rot, k_rot.T, preferred_element_type=jnp.float32)) * factor
        scores = jnp.where(causal, scores, -jnp.inf)
        highest = lax.optimization_barrier(jnp.max(scores, axis=1, keepdims=True))
        exponent = jnp.exp(scores - highest)
        probs = (exponent / lax.optimization_barrier(jnp.sum(exponent, axis=1, keepdims=True))).astype(jnp.bfloat16)
        return jnp.dot(probs, head_values, preferred_element_type=jnp.float32).astype(jnp.bfloat16)
    per_head = lax.map(one_head, (q_nope.transpose(1, 0, 2), q_rot.transpose(1, 0, 2), k_nope.transpose(1, 0, 2), values.transpose(1, 0, 2)))
    attn = per_head.transpose(1, 0, 2).reshape(length, HEADS * V)
    group_width = HEADS * V // N_TENSOR
    attn_groups = attn.reshape(length, N_TENSOR, group_width).transpose(1, 0, 2)
    weight_groups = wo.reshape(N_TENSOR, group_width, D)

    def one_group(operands):
        group_attn, group_weight = operands
        partial_sum = jnp.dot(group_attn, group_weight, preferred_element_type=jnp.float32)
        return lax.optimization_barrier(partial_sum.astype(jnp.bfloat16)).astype(jnp.float32)
    partials = lax.map(one_group, (attn_groups, weight_groups))
    return lax.optimization_barrier(jnp.sum(partials, axis=0)).astype(jnp.bfloat16)

def reference(q_latent, kv_compressed, q_gain, kv_gain, wq_b, wkv_b, wo):
    q_groups = q_latent.reshape(N_DP, SEQ, QL)
    kv_groups = kv_compressed.reshape(N_DP, SEQ, KL + R)

    def per_sequence(operands):
        return one_sequence(operands[0], operands[1], q_gain, kv_gain, wq_b, wkv_b, wo)
    mixed = lax.map(per_sequence, (q_groups, kv_groups))
    return mixed.reshape(TOKENS, D)
```

```python
import functools

import jax
import jax.numpy as jnp
import numpy as np
from jax import lax
from jax.experimental import pallas as pl
from jax.experimental.pallas import tpu as pltpu
from jax.sharding import Mesh, PartitionSpec as P

NOPE = 128
R = 64
V = 128
QL = 1536
KL = 512
SEQ = 1024
BLK = 128
EPS = 1e-06
LAT = QL + KL + 2 * R
QW = 4 * (NOPE + R)
KW = 4 * (NOPE + V)
GW = 896
AX = ("y", "xh", "core", "z", "xl")
SIZES = (4, 2, 2, 4, 2)
BF = jnp.bfloat16
F32 = jnp.float32


def rope_tables():
    half = R // 2
    freq = 10000.0 ** (-np.arange(half) / half)
    ang = np.arange(SEQ)[:, None] * freq[None, :]
    cos = np.tile(np.cos(ang), (1, 4)).astype(np.float32)
    sin = np.sin(ang)
    sin = np.concatenate([-sin, sin, -sin, sin], axis=1).astype(np.float32)
    return cos, sin


COS, SIN = rope_tables()


def pairs_of(partner):
    out = []
    for source in range(int(np.prod(SIZES))):
        place = np.unravel_index(source, SIZES)
        out.append((source, int(np.ravel_multi_index(partner(*map(int, place)), SIZES))))
    return out


def first(core):
    return 3 if core else 1


def second(core):
    return 1 if core else 3


SWAPS = {
    "core": pairs_of(lambda y, xh, c, z, xl: (y, xh, 1 - c, z, xl)),
    "xh": pairs_of(lambda y, xh, c, z, xl: (y, 1 - xh, c, z, xl)),
    "xl": pairs_of(lambda y, xh, c, z, xl: (y, xh, c, z, 1 - xl)),
    "y1": pairs_of(lambda y, xh, c, z, xl: (y ^ first(c), xh, c, z, xl)),
    "y2": pairs_of(lambda y, xh, c, z, xl: (y ^ second(c), xh, c, z, xl)),
    "z1": pairs_of(lambda y, xh, c, z, xl: (y, xh, c, z ^ first(c), xl)),
    "z2": pairs_of(lambda y, xh, c, z, xl: (y, xh, c, z ^ second(c), xl)),
}


def swap(x, which):
    return lax.ppermute(x, AX, SWAPS[which])


def lanes(shape):
    return lax.broadcasted_iota(jnp.int32, shape, len(shape) - 1)


def turn(x):
    return pltpu.roll(x, 64, x.ndim - 1)


def rope_pairs(x, cos, sin):
    low = (lanes(x.shape) // 32) % 2 == 0
    swapped = jnp.where(low, pltpu.roll(x, 96, 1), pltpu.roll(x, 32, 1))
    return x * cos + swapped * sin


def norm_kernel(place, q_ref, kv_ref, qg_ref, kvg_ref, cos_ref, sin_ref, mine_ref, theirs_ref, rows):
    def norm(x, gain):
        return x * lax.rsqrt(jnp.mean(x * x, axis=-1, keepdims=True) + EPS) * gain

    rows[:, :QL] = norm(q_ref[...].astype(F32), qg_ref[...]).astype(BF)
    rows[:, QL : QL + KL] = norm(kv_ref[:, :KL].astype(F32), kvg_ref[...]).astype(BF)
    rot = kv_ref[:, KL:].astype(F32)
    rot = rope_pairs(jnp.concatenate([rot, rot], axis=1), cos_ref[...], sin_ref[...])
    rows[:, QL + KL :] = rot.astype(BF)
    core = place[2]
    mine_ref[...] = rows[pl.ds(pl.multiple_of(core * 64, 64), 64), :]
    theirs_ref[...] = rows[pl.ds(pl.multiple_of((1 - core) * 64, 64), 64), :]


def norms(place, q_latent, kv_compressed, q_gain, kv_gain):
    half = jax.ShapeDtypeStruct((64, LAT), BF)
    whole = lambda shape: pl.BlockSpec(shape, lambda i, p: (0, 0))
    table = pl.BlockSpec((BLK, 128), lambda i, p: (p[3] * 2 + p[4], 0))
    return pl.pallas_call(
        norm_kernel,
        out_shape=(half, half),
        grid_spec=pltpu.PrefetchScalarGridSpec(
            num_scalar_prefetch=1,
            grid=(1,),
            in_specs=[
                whole((BLK, QL)),
                whole((BLK, KL + R)),
                whole((1, QL)),
                whole((1, KL)),
                table,
                table,
            ],
            out_specs=(whole((64, LAT)), whole((64, LAT))),
            scratch_shapes=[pltpu.VMEM((BLK, LAT), BF)],
        ),
        compiler_params=pltpu.CompilerParams(vmem_limit_bytes=16 * 2**20),
        cost_estimate=pl.CostEstimate(flops=2**20, bytes_accessed=2**21, transcendentals=0),
        name="norms",
    )(place, q_latent, kv_compressed, q_gain[None], kv_gain[None], COS, SIN)


def attention_kernel(
    place, m0, m1, t0, t1, wq0, wq1, wk0, wk1, cos_ref, sin_ref, o_ref, x, wq, wk, q, kv, sems
):
    y, xh, core, z, xl = (place[i] for i in range(5))
    copies = {"x": [], "wk": [], "wq": []}
    count = 0

    def start(kind, source, target):
        nonlocal count
        copy = pltpu.make_async_copy(source, target, sems.at[count])
        copy.start()
        copies[kind].append(copy)
        count += 1

    def weights(kind, near, far, target, rows):
        near_y, far_y = 1 + 2 * core, 3 - 2 * core
        for part, ys in ((near, (0, near_y)), (far, (far_y, 2))):
            for i, yr in enumerate(ys):
                for xr in range(2):
                    for cr in range(2):
                        at = ((y ^ yr) * 4 + (xh ^ xr) * 2 + (core ^ cr)) * rows
                        start(
                            kind,
                            part.at[pl.ds(((i * 2 + xr) * 2 + cr) * rows, rows)],
                            target.at[pl.ds(pl.multiple_of(at, rows), rows)],
                        )

    for half, near, far in ((core, m0, m1), (1 - core, t0, t1)):
        near_z, far_z = 1 + 2 * half, 3 - 2 * half
        for part, zs in ((near, (0, near_z)), (far, (far_z, 2))):
            for i, zr in enumerate(zs):
                for xr in range(2):
                    at = ((z ^ zr) * 2 + (xl ^ xr)) * BLK + half * 64
                    start(
                        "x",
                        part.at[pl.ds((i * 2 + xr) * 64, 64)],
                        x.at[pl.ds(pl.multiple_of(at, 64), 64)],
                    )
    weights("wk", wk0, wk1, wk, 32)
    weights("wq", wq0, wq1, wq, 96)
    for copy in copies["x"] + copies["wk"]:
        copy.wait()
    for rows in (pl.ds(0, 512), pl.ds(512, 512)):
        kv[rows, :] = jnp.dot(
            x[rows, QL : QL + KL], wk[...], preferred_element_type=F32
        ).astype(BF)
    for copy in copies["wq"]:
        copy.wait()
    for block in range(4):
        rows = pl.ds(block * 256, 256)
        full = jnp.dot(x[rows, :QL], wq[...], preferred_element_type=F32)
        cos, sin = cos_ref[rows, :], sin_ref[rows, :]
        low = lanes((256, 128)) < 64
        for pair in range(2):
            a, b, c = (full[:, (pair * 3 + i) * 128 : (pair * 3 + i + 1) * 128] for i in range(3))
            rot = rope_pairs(jnp.where(low, b, c), cos, sin).astype(BF)
            other = jnp.where(low, turn(b), turn(c))
            q[rows, pair * 512 : pair * 512 + 128] = a.astype(BF)
            q[rows, pair * 512 + 128 : pair * 512 + 256] = rot
            q[rows, pair * 512 + 256 : pair * 512 + 384] = other.astype(BF)
            q[rows, pair * 512 + 384 : pair * 512 + 512] = rot
    twice = x[:, QL + KL :]
    half_lane = lanes((SEQ, 128)) < 64
    nothing = jnp.zeros_like(twice)
    rots = (jnp.where(half_lane, twice, nothing), jnp.where(half_lane, nothing, twice))
    factor = np.float32(np.log2(np.e) / np.sqrt(NOPE + R))
    causal = lax.broadcasted_iota(jnp.int32, (256, 256), 0) >= lanes((256, 256))
    for head in range(4):
        keys = jnp.concatenate([kv[:, head * 256 : head * 256 + 128], rots[head % 2]], axis=1)
        for block in range(4):
            length = (block + 1) * 256
            queries = q[block * 256 : (block + 1) * 256, head * 256 : (head + 1) * 256]
            scores = lax.dot_general(
                queries, keys[:length], (((1,), (1,)), ((), ())), preferred_element_type=F32
            )
            last = jnp.where(causal, scores[:, length - 256 :], -jnp.inf)
            if block:
                scores = jnp.concatenate([scores[:, : length - 256], last], axis=1)
            else:
                scores = last
            highest = jnp.max(scores, axis=1, keepdims=True)
            weight = jnp.exp2((scores - highest) * factor)
            total = jnp.sum(weight, axis=1, keepdims=True)
            out = jnp.dot(
                weight.astype(BF),
                kv[:length, head * 256 + 128 : (head + 1) * 256],
                preferred_element_type=F32,
            )
            o_ref[block * 256 : (block + 1) * 256, head * V : (head + 1) * V] = (
                out / total
            ).astype(BF)


def attention(place, latents, wq, wk):
    anywhere = pl.BlockSpec(memory_space=pl.ANY)
    whole = lambda shape: pl.BlockSpec(shape, lambda i, p: (0, 0))
    return pl.pallas_call(
        attention_kernel,
        out_shape=jax.ShapeDtypeStruct((SEQ, 4 * V), BF),
        grid_spec=pltpu.PrefetchScalarGridSpec(
            num_scalar_prefetch=1,
            grid=(1,),
            in_specs=[anywhere] * 8 + [whole((SEQ, 128))] * 2,
            out_specs=whole((SEQ, 4 * V)),
            scratch_shapes=[
                pltpu.VMEM((SEQ, LAT), BF),
                pltpu.VMEM((QL, QW), BF),
                pltpu.VMEM((KL, KW), BF),
                pltpu.VMEM((SEQ, 1024), BF),
                pltpu.VMEM((SEQ, KW), BF),
                pltpu.SemaphoreType.DMA((48,)),
            ],
        ),
        compiler_params=pltpu.CompilerParams(vmem_limit_bytes=40 * 2**20),
        cost_estimate=pl.CostEstimate(
            flops=16 * 10**9, bytes_accessed=9 * 2**20, transcendentals=3 * 2**20
        ),
        name="attention",
    )(place, *latents, *wq, *wk, COS, SIN)


def project_kernel(x_first, place, own, other, w_ref, send_ref, keep_ref, a, sems):
    core, z, xl = place[2], place[3], place[4]
    near, far = 1 + 2 * core, 3 - 2 * core
    if x_first:
        order = [(zr, xr) for xr in (1, 0) for zr in (0, far, near, 2)]
    else:
        order = [(zr, xr) for zr in (near, 2, 0, far) for xr in (0, 1)]
    copies = []
    for slot, (zr, xr) in enumerate(order):
        rows = pl.ds(pl.multiple_of(((z ^ zr) * 2 + (xl ^ xr)) * BLK, BLK), BLK)
        for i, (part, owner) in enumerate(((own, core), (other, 1 - core))):
            columns = pl.ds(pl.multiple_of(owner * 512, 512), 512)
            copy = pltpu.make_async_copy(
                part.at[rows],
                a.at[pl.ds(slot * BLK, BLK), columns],
                sems.at[slot * 2 + i],
            )
            copy.start()
            copies.append(copy)
    for half, ref in ((0, send_ref), (1, keep_ref)):
        for copy in copies[half * 8 : half * 8 + 8]:
            copy.wait()
        ref[...] = jnp.dot(
            a[half * 512 : half * 512 + 512, :], w_ref[...], preferred_element_type=F32
        ).astype(BF)


def project(place, own, other, weight, x_first):
    anywhere = pl.BlockSpec(memory_space=pl.ANY)
    whole = lambda shape: pl.BlockSpec(shape, lambda i, p: (0, 0))
    half = jax.ShapeDtypeStruct((512, GW), BF)
    return pl.pallas_call(
        functools.partial(project_kernel, x_first),
        out_shape=(half, half),
        grid_spec=pltpu.PrefetchScalarGridSpec(
            num_scalar_prefetch=1,
            grid=(1,),
            in_specs=[anywhere, anywhere, whole((SEQ, GW))],
            out_specs=(whole((512, GW)), whole((512, GW))),
            scratch_shapes=[pltpu.VMEM((SEQ, SEQ), BF), pltpu.SemaphoreType.DMA((16,))],
        ),
        compiler_params=pltpu.CompilerParams(vmem_limit_bytes=24 * 2**20),
        cost_estimate=pl.CostEstimate(
            flops=2 * SEQ * SEQ * GW, bytes_accessed=6 * 2**20, transcendentals=0
        ),
        name="project",
    )(place, own, other, weight)


def added(x, y):
    return (x.astype(F32) + y.astype(F32)).astype(BF)


def summed(send, keep, x_first):
    for which in ("xl", "z1", "z2") if x_first else ("z1", "z2", "xl"):
        came = swap(send, which)
        rows = keep.shape[0] // 2
        if rows >= BLK:
            send = added(keep[rows:], came[rows:])
            keep = added(keep[:rows], came[:rows])
        else:
            keep = added(keep, came)
    return keep


def collect_kernel(place, *refs):
    own, other, o_ref = refs[:4], refs[4:8], refs[8]
    y, core = place[0], place[2]
    low = lanes((BLK, 128)) < 64
    for g, h, yr in ((0, 0, 0), (1, 2, 1 + 2 * core), (2, 1, 3 - 2 * core), (3, 3, 2)):
        mine, its = own[g][...].astype(F32), other[h][...].astype(F32)
        a, b = jnp.where(core == 0, mine, its), jnp.where(core == 0, its, mine)
        a = [a[:, i * 128 : (i + 1) * 128] for i in range(7)]
        b = [b[:, i * 128 : (i + 1) * 128] for i in range(7)]
        ta, tb = [turn(t) for t in a], [turn(t) for t in b]
        pick = lambda s, t: jnp.where(low, s, t)
        row = a[:3] + [pick(a[3], tb[0])]
        row += [pick(tb[i], tb[i + 1]) for i in range(3)]
        row += [pick(ta[i], ta[i + 1]) for i in range(3, 6)]
        row += [pick(ta[6], b[3])] + b[4:]
        at = pl.multiple_of((y ^ yr) * 2 * GW, 2 * GW)
        o_ref[:, pl.ds(at, 2 * GW)] = jnp.concatenate(row, axis=1).astype(BF)


def collect(place, own, other):
    whole = lambda shape: pl.BlockSpec(shape, lambda i, p: (0, 0))
    return pl.pallas_call(
        collect_kernel,
        out_shape=jax.ShapeDtypeStruct((BLK, 8 * GW), BF),
        grid_spec=pltpu.PrefetchScalarGridSpec(
            num_scalar_prefetch=1,
            grid=(1,),
            in_specs=[whole((BLK, GW))] * 8,
            out_specs=whole((BLK, 8 * GW)),
        ),
        compiler_params=pltpu.CompilerParams(vmem_limit_bytes=24 * 2**20),
        cost_estimate=pl.CostEstimate(flops=2**20, bytes_accessed=2**22, transcendentals=0),
        name="collect",
    )(place, *own, *other)


def doubled(x, which):
    return jnp.concatenate([x, swap(x, which)], axis=0)


def shards(q_latent, kv_compressed, q_gain, kv_gain, wq_b, wkv_b, wo):
    place = jnp.stack([lax.axis_index(a) for a in AX]).astype(jnp.int32)
    core, xh = place[2], place[1]

    def split(w, width):
        mine = lax.dynamic_slice_in_dim(w, core * width, width, 1)
        theirs = lax.dynamic_slice_in_dim(w, (1 - core) * width, width, 1)
        return mine, theirs

    def gathered(w, width):
        mine, theirs = split(w, width)
        w = jnp.concatenate([mine, swap(theirs, "core")], axis=0)
        near = doubled(doubled(w, "xh"), "y1")
        return near, swap(near, "y2")

    mine, theirs = norms(place, q_latent, kv_compressed, q_gain, kv_gain)
    theirs = swap(theirs, "core")
    starts = (jnp.where(core == 0, mine, theirs), jnp.where(core == 0, theirs, mine))

    wk = gathered(wkv_b, KW)
    wq = gathered(wq_b, QW)

    own, other = [], []
    for rows in starts:
        near = doubled(doubled(rows, "xl"), "z1")
        far = swap(near, "z2")
        latents = (near, far, swap(near, "core"), swap(far, "core"))
        out = attention(place, latents, wq, wk)
        own.append(out)
        other.append(swap(out, "core"))

    far_wo = swap(wo, "xh")
    w0 = jnp.where(
        xh == 0, jnp.concatenate([wo, far_wo], axis=1), jnp.concatenate([far_wo, wo], axis=1)
    )
    w1 = swap(w0, "y1")
    w2 = swap(w0, "y2")
    w3 = swap(w1, "y2")
    parts = [[None] * 4, [None] * 4]
    for s, g in ((0, 0), (0, 1), (1, 0), (1, 1), (0, 2), (1, 2), (0, 3), (1, 3)):
        x_first = g in (1, 2) if s == 0 else g == 1
        send, keep = project(place, own[s], other[s], (w0, w1, w2, w3)[g], x_first)
        parts[s][g] = summed(send, keep, x_first)
    mine = [jnp.where(core == 0, a, b) for a, b in zip(*parts)]
    theirs = [swap(jnp.where(core == 0, b, a), "core") for a, b in zip(*parts)]
    return collect(place, mine, theirs)


def solution(mesh):
    parts = Mesh(mesh.devices.reshape(SIZES), AX)
    dp, tensor = AX[:3], AX[3:]
    in_specs = (
        P(AX, None),
        P(AX, None),
        P(),
        P(),
        P(dp, tensor),
        P(dp, tensor),
        P(tensor, dp),
    )
    return jax.shard_map(
        shards, mesh=parts, in_specs=in_specs, out_specs=P(AX, None), check_vma=False
    )
```

```python
import functools

import jax
import jax.numpy as jnp
import numpy as np
from jax import lax
from jax.experimental import pallas as pl
from jax.experimental.pallas import tpu as pltpu
from jax.sharding import Mesh, PartitionSpec as P

NOPE = 128
R = 64
V = 128
QL = 1536
KL = 512
SEQ = 1024
BLK = 128
EPS = 1e-06
LAT = QL + KL + 2 * R
QW = 4 * (NOPE + R)
KW = 4 * (NOPE + V)
GW = 896
AX = ("y", "xh", "core", "z", "xl")
SIZES = (4, 2, 2, 4, 2)
PIECE = 288
BF = jnp.bfloat16
F32 = jnp.float32


def rope_tables():
    half = R // 2
    freq = 10000.0 ** (-np.arange(half) / half)
    ang = np.arange(SEQ)[:, None] * freq[None, :]
    cos = np.tile(np.cos(ang), (1, 4)).astype(np.float32)
    sin = np.sin(ang)
    sin = np.concatenate([-sin, sin, -sin, sin], axis=1).astype(np.float32)
    return cos, sin


COS, SIN = rope_tables()


def pairs_of(partner):
    out = []
    for source in range(int(np.prod(SIZES))):
        place = np.unravel_index(source, SIZES)
        out.append((source, int(np.ravel_multi_index(partner(*map(int, place)), SIZES))))
    return out


MOVES = {
    "x": lambda y, xh, c, z, xl: (y, xh, c, z, 1 - xl),
    "p": lambda y, xh, c, z, xl: (y, xh, c, z ^ 1, xl),
    "q": lambda y, xh, c, z, xl: (y, xh, c, z ^ 3, xl),
    "h": lambda y, xh, c, z, xl: (y, 1 - xh, c, z, xl),
    "r": lambda y, xh, c, z, xl: (y ^ 1, xh, c, z, xl),
    "s": lambda y, xh, c, z, xl: (y ^ 3, xh, c, z, xl),
    "c": lambda y, xh, c, z, xl: (y, xh, 1 - c, z, xl),
}
RING = {"x": 0, "h": 0, "p": 1, "r": 1, "q": 3, "s": 3}
PAIR = {"x": 1, "h": 1, "p": 0, "r": 0, "q": 0, "s": 0}


@functools.cache
def swap_pairs(moves):
    return pairs_of(lambda *at: MOVES[moves[0] if at[2] == 0 else moves[-1]](*at))


def swap(x, which):
    return lax.ppermute(x, AX, swap_pairs(which))


def steps_of(path, core):
    def choose(a, b):
        return a if a == b else jnp.where(core == 0, a, b)

    return [
        (choose(RING[m[0]], RING[m[-1]]), choose(PAIR[m[0]], PAIR[m[-1]])) for m in path
    ]


def corners(steps):
    out = [(0, 0)]
    for ring, pair in steps:
        out = [(r ^ dr, x ^ dx) for r, x in out for dr, dx in ((0, 0), (ring, pair))]
    return out


def lanes(shape):
    return lax.broadcasted_iota(jnp.int32, shape, len(shape) - 1)


def turn(x):
    return pltpu.roll(x, 64, x.ndim - 1)


def rope_pairs(x, cos, sin):
    low = (lanes(x.shape) // 32) % 2 == 0
    swapped = jnp.where(low, pltpu.roll(x, 96, 1), pltpu.roll(x, 32, 1))
    return x * cos + swapped * sin


ANYWHERE = pl.BlockSpec(memory_space=pl.ANY)
FAR = pl.BlockSpec(memory_space=pltpu.HBM)
PLACE = pl.BlockSpec(memory_space=pltpu.SMEM)
LOCAL = pl.BlockSpec(memory_space=pltpu.VMEM)
WIDE = 60 * 2**20


def cost(name):
    return pl.CostEstimate(
        flops=int(COSTS.get(name, 1) * 10**9), bytes_accessed=2**20, transcendentals=0
    )


def copied(pairs, sems):
    copies = [pltpu.make_async_copy(a, b, sems.at[i]) for i, (a, b) in enumerate(pairs)]
    for copy in copies:
        copy.start()
    return copies


def cut_kernel(place, wk_hbm, wq_hbm, mine, theirs, wk, wq, sems):
    core = place[2]
    for copy in copied(((wk_hbm, wk), (wq_hbm, wq)), sems):
        copy.wait()
    for which, ref in ((1 - core, theirs), (core, mine)):
        at = pl.multiple_of(which * QW, QW)
        ref[:96] = wq[:, pl.ds(at, QW)]
        at = pl.multiple_of(which * KW, KW)
        ref[96:128] = wk[:, pl.ds(at, QW)]
        at = pl.multiple_of(which * KW + QW, KW - QW)
        rest = wk[:, pl.ds(at, KW - QW)]
        ref[128:160] = jnp.concatenate([rest, jnp.zeros((32, 512), BF)], axis=1)


def cut(place, wk, wq):
    out = jax.ShapeDtypeStruct((160, QW), BF)
    return pl.pallas_call(
        cut_kernel,
        out_shape=(out, out),
        in_specs=[PLACE] + [FAR] * 2,
        scratch_shapes=[
            pltpu.VMEM(wk.shape, BF),
            pltpu.VMEM(wq.shape, BF),
            pltpu.SemaphoreType.DMA((2,)),
        ],
        compiler_params=pltpu.CompilerParams(vmem_limit_bytes=WIDE),
        cost_estimate=cost("cut"),
        name="cut",
    )(place, wk, wq)


def pair_kernel(place, mine, came, after, out):
    core = place[2]
    for which, ref in ((core, mine), (1 - core, came)):
        out[pl.ds(pl.multiple_of(which * 96, 96), 96)] = ref[:96]
        out[pl.ds(pl.multiple_of(192 + which * 32, 32), 32)] = ref[96:128]
        at = pl.multiple_of(which * 256, 256)
        out[256:288, pl.ds(at, 256)] = ref[128:160, :256]
    out[256:288, 512:] = jnp.zeros((32, 256), BF)


def pair(place, mine, came, after):
    return pl.pallas_call(
        pair_kernel,
        out_shape=jax.ShapeDtypeStruct((PIECE, QW), BF),
        in_specs=[PLACE, LOCAL, LOCAL, ANYWHERE],
        compiler_params=pltpu.CompilerParams(vmem_limit_bytes=16 * 2**20),
        cost_estimate=cost("pair"),
        name="pair",
    )(place, mine, came, after)


def sort_kernel(place, mine, came, after, first, second):
    zero = place[2] == 0
    first[...] = jnp.where(zero, mine[...], came[...])
    second[...] = jnp.where(zero, came[...], mine[...])


def sort(place, mine, came, after):
    return pl.pallas_call(
        sort_kernel,
        out_shape=(jax.ShapeDtypeStruct(mine.shape, BF),) * 2,
        in_specs=[PLACE, LOCAL, LOCAL, ANYWHERE],
        compiler_params=pltpu.CompilerParams(vmem_limit_bytes=16 * 2**20),
        cost_estimate=cost("sort"),
        name="sort",
    )(place, mine, came, after)


def take_kernel(x, after, out):
    out[...] = x[...]


def take(x, after):
    return pl.pallas_call(
        take_kernel,
        out_shape=jax.ShapeDtypeStruct(x.shape, BF),
        in_specs=[LOCAL, ANYWHERE],
        compiler_params=pltpu.CompilerParams(vmem_limit_bytes=16 * 2**20),
        cost_estimate=cost("take"),
        name="take",
    )(x, after)


def join_kernel(a, b, after, out):
    out[: a.shape[0]] = a[...]
    out[a.shape[0] :] = b[...]


def join(a, b, after):
    return pl.pallas_call(
        join_kernel,
        out_shape=jax.ShapeDtypeStruct((2 * a.shape[0], a.shape[1]), BF),
        in_specs=[LOCAL, LOCAL, ANYWHERE],
        compiler_params=pltpu.CompilerParams(vmem_limit_bytes=16 * 2**20),
        cost_estimate=cost("join"),
        name="join",
    )(a, b, after)


def touch_kernel(x, after, out):
    out[...] = jnp.zeros_like(out)


def touch(x, after, name):
    return pl.pallas_call(
        touch_kernel,
        out_shape=jax.ShapeDtypeStruct((16, 128), BF),
        in_specs=[ANYWHERE, ANYWHERE],
        cost_estimate=cost(name),
        name="touch",
    )(x, after)


def norm_kernel(
    place, q_hbm, kv_hbm, qg_hbm, kvg_hbm, cos_hbm, sin_hbm, after, mine_ref, theirs_ref,
    rows, q_ref, kv_ref, qg_ref, kvg_ref, cos_ref, sin_ref, sems,
):
    core = place[2]
    at = pl.ds(pl.multiple_of((place[3] * 2 + place[4]) * BLK, BLK), BLK)
    copies = copied(
        (
            (q_hbm, q_ref),
            (kv_hbm, kv_ref),
            (qg_hbm, qg_ref),
            (kvg_hbm, kvg_ref),
            (cos_hbm.at[at], cos_ref),
            (sin_hbm.at[at], sin_ref),
        ),
        sems,
    )
    for copy in copies:
        copy.wait()

    def norm(x, gain):
        return x * lax.rsqrt(jnp.mean(x * x, axis=-1, keepdims=True) + EPS) * gain

    kv = kv_ref[...].astype(F32).T
    rows[:, :QL] = norm(q_ref[...].astype(F32), qg_ref[...][None, :]).astype(BF)
    rows[:, QL : QL + KL] = norm(kv[:, :KL], kvg_ref[...][None, :]).astype(BF)
    rot = kv[:, KL:]
    rot = rope_pairs(jnp.concatenate([rot, rot], axis=1), cos_ref[...], sin_ref[...])
    rows[:, QL + KL :] = rot.astype(BF)
    mine_ref[...] = rows[pl.ds(pl.multiple_of(core * 64, 64), 64), :]
    theirs_ref[...] = rows[pl.ds(pl.multiple_of((1 - core) * 64, 64), 64), :]


def norms(place, q_latent, kv_compressed, q_gain, kv_gain, after):
    half = jax.ShapeDtypeStruct((64, LAT), BF)
    return pl.pallas_call(
        norm_kernel,
        out_shape=(half, half),
        in_specs=[PLACE] + [FAR] * 6 + [ANYWHERE],
        scratch_shapes=[
            pltpu.VMEM((BLK, LAT), BF),
            pltpu.VMEM((BLK, QL), BF),
            pltpu.VMEM((KL + R, BLK), BF),
            pltpu.VMEM((QL,), F32),
            pltpu.VMEM((KL,), F32),
            pltpu.VMEM((BLK, 128), F32),
            pltpu.VMEM((BLK, 128), F32),
            pltpu.SemaphoreType.DMA((6,)),
        ],
        compiler_params=pltpu.CompilerParams(vmem_limit_bytes=WIDE),
        cost_estimate=cost("norms"),
        name="norms",
    )(place, q_latent, kv_compressed.T, q_gain, kv_gain, COS, SIN, after)


def attention_kernel(
    paths, place, m0, m1, t0, *refs
):
    t1, refs = refs[:PIECES], refs[PIECES:]
    w0, w1, after, cos_hbm, sin_hbm, o0_ref, o1_ref = refs[:7]
    x, wq, wk, cos_ref, sin_ref, q, kv, sems = refs[7:]
    y, xh, core, z, xl = (place[i] for i in range(5))
    copies = {"x": [], "wk": [], "wq": []}
    count = 0

    def start(kind, source, target):
        nonlocal count
        copy = pltpu.make_async_copy(source, target, sems.at[count])
        copy.start()
        copies[kind].append(copy)
        count += 1

    def blocks(path, owner, near, far):
        first, second, third = steps_of(path, owner)
        for i, (ring, pair) in enumerate(corners((second, first))):
            yield near, i, ring, pair
            yield far, i, ring ^ third[0], pair ^ third[1]

    for half, near, far in ((core, m0, m1), (1 - core, t0, t1)):
        for part, i, zr, xr in blocks(paths[0], half, near, far):
            if isinstance(part, tuple):
                size = 4 // PIECES
                part, i = part[i // size], i % size
            at = ((z ^ zr) * 2 + (xl ^ xr)) * BLK + half * 64
            start("x", part.at[pl.ds(i * 64, 64)], x.at[pl.ds(pl.multiple_of(at, 64), 64)])
    for part, i, yr, xr in blocks(paths[1], core, w0, w1):
        at = (y ^ yr) * 2 + (xh ^ xr)
        rows = pl.ds(pl.multiple_of(at * 64, 64), 64)
        start("wk", part.at[pl.ds(i * PIECE + 192, 64)], wk.at[rows, pl.ds(0, QW)])
        for c in range(2):
            start(
                "wk",
                part.at[pl.ds(i * PIECE + 256, 32), pl.ds(c * 256, 256)],
                wk.at[pl.ds(pl.multiple_of(at * 64 + c * 32, 32), 32), pl.ds(QW, 256)],
            )
    for part, i, yr, xr in blocks(paths[1], core, w0, w1):
        at = (y ^ yr) * 2 + (xh ^ xr)
        rows = pl.ds(pl.multiple_of(at * 192, 192), 192)
        start("wq", part.at[pl.ds(i * PIECE, 192)], wq.at[rows])
    start("wq", cos_hbm, cos_ref)
    start("wq", sin_hbm, sin_ref)
    for copy in copies["x"] + copies["wk"]:
        copy.wait()
    for rows in (pl.ds(0, 512), pl.ds(512, 512)):
        kv[rows, :] = jnp.dot(
            x[rows, QL : QL + KL], wk[...], preferred_element_type=F32
        ).astype(BF)
    for copy in copies["wq"]:
        copy.wait()
    for block in range(4):
        rows = pl.ds(block * 256, 256)
        full = jnp.dot(x[rows, :QL], wq[...], preferred_element_type=F32)
        cos, sin = cos_ref[rows, :], sin_ref[rows, :]
        low = lanes((256, 128)) < 64
        for pair in range(2):
            a, b, c = (full[:, (pair * 3 + i) * 128 : (pair * 3 + i + 1) * 128] for i in range(3))
            rot = rope_pairs(jnp.where(low, b, c), cos, sin).astype(BF)
            other = jnp.where(low, turn(b), turn(c))
            q[rows, pair * 512 : pair * 512 + 128] = a.astype(BF)
            q[rows, pair * 512 + 128 : pair * 512 + 256] = rot
            q[rows, pair * 512 + 256 : pair * 512 + 384] = other.astype(BF)
            q[rows, pair * 512 + 384 : pair * 512 + 512] = rot
    twice = x[:, QL + KL :]
    half_lane = lanes((SEQ, 128)) < 64
    nothing = jnp.zeros_like(twice)
    rots = (jnp.where(half_lane, twice, nothing), jnp.where(half_lane, nothing, twice))
    factor = np.float32(np.log2(np.e) / np.sqrt(NOPE + R))
    causal = lax.broadcasted_iota(jnp.int32, (256, 256), 0) >= lanes((256, 256))
    def scores_of(head, block):
        length = (block + 1) * 256
        rows = slice(block * 256, length)
        return jnp.dot(
            q[rows, head * 256 : (head + 1) * 256],
            keys[head][:, :length],
            preferred_element_type=F32,
        )

    keys = []
    for head in range(4):
        own = jnp.concatenate([kv[:, head * 256 : head * 256 + 128], rots[head % 2]], axis=1)
        keys.append(own.T)
    tasks = [(head, block) for head in range(4) for block in range(4)]
    coming = scores_of(*tasks[0])
    for i, (head, block) in enumerate(tasks):
        scores = coming
        if i + 1 < len(tasks):
            coming = scores_of(*tasks[i + 1])
        length = (block + 1) * 256
        last = jnp.where(causal, scores[:, length - 256 :], -jnp.inf)
        if block:
            scores = jnp.concatenate([scores[:, : length - 256], last], axis=1)
        else:
            scores = last
        highest = jnp.max(scores, axis=1, keepdims=True)
        weight = jnp.exp2((scores - highest) * factor)
        total = jnp.sum(weight, axis=1, keepdims=True)
        out = jnp.dot(
            weight.astype(BF),
            kv[:length, head * 256 + 128 : (head + 1) * 256],
            preferred_element_type=F32,
        )
        column = head % 2 * V
        (o0_ref, o1_ref)[head // 2][block * 256 : length, column : column + V] = (
            out / total
        ).astype(BF)


def attention(place, paths, latents, weights, after):
    return pl.pallas_call(
        functools.partial(attention_kernel, paths),
        out_shape=(jax.ShapeDtypeStruct((SEQ, 2 * V), BF),) * 2,
        in_specs=[PLACE] + [ANYWHERE] * (8 + PIECES),
        scratch_shapes=[
            pltpu.VMEM((SEQ, LAT), BF),
            pltpu.VMEM((QL, QW), BF),
            pltpu.VMEM((KL, KW), BF),
            pltpu.VMEM((SEQ, 128), F32),
            pltpu.VMEM((SEQ, 128), F32),
            pltpu.VMEM((SEQ, 1024), BF),
            pltpu.VMEM((SEQ, KW), BF),
            pltpu.SemaphoreType.DMA((50,)),
        ],
        compiler_params=pltpu.CompilerParams(vmem_limit_bytes=40 * 2**20),
        cost_estimate=cost("attention"),
        name="attention",
    )(place, *latents, *weights, after, COS, SIN)


def project_kernel(path, place, own0, own1, other0, other1, w_hbm, after, send_ref, keep_ref, a, w, sems):
    xh, core, z, xl = (place[i] for i in range(1, 5))
    order = corners(steps_of(path, core))
    order = order[4:] + order[:4]
    pairs = []
    for r in range(2):
        at = pl.multiple_of((xh ^ r) * 448, 448)
        pairs.append((w_hbm.at[pl.ds(r * 448, 448)], w.at[pl.ds(at, 448)]))
    for slot, (zr, xr) in enumerate(order):
        rows = pl.ds(pl.multiple_of(((z ^ zr) * 2 + (xl ^ xr)) * BLK, BLK), BLK)
        for owner, parts in ((core, (own0, own1)), (1 - core, (other0, other1))):
            for i, part in enumerate(parts):
                columns = pl.ds(pl.multiple_of(owner * 512 + i * 256, 256), 256)
                pairs.append((part.at[rows], a.at[pl.ds(slot * BLK, BLK), columns]))
    copies = copied(pairs, sems)
    for half, ref in ((0, send_ref), (1, keep_ref)):
        for copy in copies[half * 18 : half * 16 + 18]:
            copy.wait()
        ref[...] = lax.dot_general(
            a[half * 512 : half * 512 + 512, :],
            w[...],
            (((1,), (1,)), ((), ())),
            preferred_element_type=F32,
        ).astype(BF)


def project(place, path, own, other, weight, after):
    half = jax.ShapeDtypeStruct((512, GW), BF)
    return pl.pallas_call(
        functools.partial(project_kernel, path),
        out_shape=(half, half),
        in_specs=[PLACE] + [ANYWHERE] * 6,
        scratch_shapes=[
            pltpu.VMEM((SEQ, SEQ), BF),
            pltpu.VMEM((GW, SEQ), BF),
            pltpu.SemaphoreType.DMA((34,)),
        ],
        compiler_params=pltpu.CompilerParams(vmem_limit_bytes=24 * 2**20),
        cost_estimate=cost("project"),
        name="project",
    )(place, *own, *other, weight, after)


def total_of(keep, came):
    return (keep.astype(F32) + came.astype(F32)).astype(BF)


def add_kernel(keep, came, after, stay, send):
    total = total_of(keep[...], came[...])
    stay[...] = total[:256]
    send[...] = total[256:]


def add(keep, came, after):
    out = jax.ShapeDtypeStruct((256, GW), BF)
    return pl.pallas_call(
        add_kernel,
        out_shape=(out, out),
        in_specs=[LOCAL, LOCAL, ANYWHERE],
        compiler_params=pltpu.CompilerParams(vmem_limit_bytes=16 * 2**20),
        cost_estimate=cost("add"),
        name="add",
    )(keep, came, after)


def add_pair_kernel(stay0, send0, keep1, came1, after, stay, send):
    total = total_of(keep1[...], came1[...])
    stay[:256] = stay0[...]
    send[:256] = send0[...]
    stay[256:] = total[:256]
    send[256:] = total[256:]


def add_pair(stay0, send0, keep1, came1, after):
    out = jax.ShapeDtypeStruct((512, GW), BF)
    return pl.pallas_call(
        add_pair_kernel,
        out_shape=(out, out),
        in_specs=[LOCAL] * 4 + [ANYWHERE],
        compiler_params=pltpu.CompilerParams(vmem_limit_bytes=24 * 2**20),
        cost_estimate=cost("add_pair"),
        name="add_pair",
    )(stay0, send0, keep1, came1, after)


def add_second_kernel(keep, came, earlier0, earlier1, after, stay, send0, send1):
    for i, (earlier, send) in enumerate(((earlier0, send0), (earlier1, send1))):
        total = total_of(keep[i * 256 : (i + 1) * 256], came[i * 256 : (i + 1) * 256])
        stay[i * BLK : (i + 1) * BLK] = total[:BLK]
        if earlier is None:
            send[...] = total[BLK:]
        else:
            send[:BLK] = earlier[...]
            send[BLK:] = total[BLK:]


def add_second(keep, came, earlier, after):
    rows = BLK * (1 + bool(earlier))
    kernel = add_second_kernel
    if not earlier:
        kernel = lambda keep, came, *refs: add_second_kernel(keep, came, None, None, *refs)
    return pl.pallas_call(
        kernel,
        out_shape=[jax.ShapeDtypeStruct((n, GW), BF) for n in (256, rows, rows)],
        in_specs=[LOCAL] * (2 + len(earlier)) + [ANYWHERE],
        compiler_params=pltpu.CompilerParams(vmem_limit_bytes=24 * 2**20),
        cost_estimate=cost("add_second"),
        name="add_second",
    )(keep, came, *earlier, after)


def add_last_kernel(place, stay0, stay1, came0, came1, after, mine, theirs):
    zero = place[2] == 0
    for i, came in enumerate((came0, came1)):
        rows = slice(i * BLK, (i + 1) * BLK)
        first = total_of(stay0[rows], came[:BLK])
        second = total_of(stay1[rows], came[BLK:])
        mine[rows] = jnp.where(zero, first, second)
        theirs[rows] = jnp.where(zero, second, first)


def add_last(place, stay0, stay1, came0, came1, after):
    out = jax.ShapeDtypeStruct((256, GW), BF)
    return pl.pallas_call(
        add_last_kernel,
        out_shape=(out, out),
        in_specs=[PLACE] + [LOCAL] * 4 + [ANYWHERE],
        compiler_params=pltpu.CompilerParams(vmem_limit_bytes=24 * 2**20),
        cost_estimate=cost("add_last"),
        name="add_last",
    )(place, stay0, stay1, came0, came1, after)


def collect_kernel(place, own0, own1, other0, other1, o_ref):
    own, other = (own0, own1), (other0, other1)
    y, core = place[0], place[2]
    low = lanes((BLK, 128)) < 64
    for g, h, yr in ((0, 0, 0), (1, 2, 1 + 2 * core), (2, 1, 3 - 2 * core), (3, 3, 2)):
        mine = own[g // 2][g % 2 * BLK : (g % 2 + 1) * BLK].astype(F32)
        its = other[h // 2][h % 2 * BLK : (h % 2 + 1) * BLK].astype(F32)
        a, b = jnp.where(core == 0, mine, its), jnp.where(core == 0, its, mine)
        a = [a[:, i * 128 : (i + 1) * 128] for i in range(7)]
        b = [b[:, i * 128 : (i + 1) * 128] for i in range(7)]
        ta, tb = [turn(t) for t in a], [turn(t) for t in b]
        pick = lambda s, t: jnp.where(low, s, t)
        row = a[:3] + [pick(a[3], tb[0])]
        row += [pick(tb[i], tb[i + 1]) for i in range(3)]
        row += [pick(ta[i], ta[i + 1]) for i in range(3, 6)]
        row += [pick(ta[6], b[3])] + b[4:]
        at = pl.multiple_of((y ^ yr) * 2 * GW, 2 * GW)
        o_ref[:, pl.ds(at, 2 * GW)] = jnp.concatenate(row, axis=1).astype(BF)


def collect(place, *parts):
    whole = lambda shape: pl.BlockSpec(shape, lambda i, p: (0, 0))
    return pl.pallas_call(
        collect_kernel,
        out_shape=jax.ShapeDtypeStruct((BLK, 8 * GW), BF),
        grid_spec=pltpu.PrefetchScalarGridSpec(
            num_scalar_prefetch=1,
            grid=(1,),
            in_specs=[whole((2 * BLK, GW))] * 4,
            out_specs=whole((BLK, 8 * GW)),
        ),
        compiler_params=pltpu.CompilerParams(vmem_limit_bytes=24 * 2**20),
        cost_estimate=cost("collect"),
        name="collect",
    )(place, *parts)


LATENT_PATHS = (("x", "pq", "qp"), ("x", "pq", "qp"))
WEIGHT_PATH = ("h", "rs", "sr")
SUM_PATHS = (("xp", "qx", "pq"), ("pq", "qx", "xp"), ("qx", "pq", "xp"), ("xp", "pq", "qx"))
ORDER = (
    *("w", "a", "b", "take", "w", "a", "b", "o", "A0", "P00", "P01", "A1", "+00", "+01",),
    *("P10", "P11", "P02", "P03", "P12", "P13", "*00", "+10", "+11", "+02", "+03", "+12", "+13", "*10",),
    *("*02", "*12",),
)
COSTS = {"project": 2, "attention": 4, "take": 9, "join": 6}
NORMS_FIRST = False
PIECES = 1


def shards(q_latent, kv_compressed, q_gain, kv_gain, wq_b, wkv_b, wo):
    place = jnp.stack([lax.axis_index(a) for a in AX]).astype(jnp.int32)
    core, xh = place[2], place[1]

    mine_w, theirs_w = cut(place, wkv_b, wq_b)
    came_w = swap(theirs_w, "c")
    if NORMS_FIRST:
        mine, theirs = norms(place, q_latent, kv_compressed, q_gain, kv_gain, mine_w)
        w = last = pair(place, mine_w, came_w, mine)
        came = swap(theirs, "c")
    else:
        w = pair(place, mine_w, came_w, mine_w)
        mine, theirs = norms(place, q_latent, kv_compressed, q_gain, kv_gain, w)
        came = swap(theirs, "c")
        last = mine
    w_came = swap(w, WEIGHT_PATH[0])
    w_hops = list(WEIGHT_PATH[1:])
    a, b = sort(place, mine, came, last)
    last = a
    hops = {"a": list(LATENT_PATHS[0]), "b": list(LATENT_PATHS[1])}
    blocks = {"a": (a, swap(a, hops["a"].pop(0))), "b": (b, swap(b, hops["b"].pop(0)))}

    def spread(near, far):
        size = far.shape[0] // PIECES
        parts = [swap(far[i * size : (i + 1) * size], "c") for i in range(PIECES)]
        return (near, far, swap(near, "c"), *parts)

    latents, own, other, weights = [], [], [], []
    sums, stays, kept, thirds = {}, {}, {}, {}
    for step in ORDER:
        kind, s = step[0], int(step[1]) if step[-1].isdigit() else 0
        if step == "w":
            w = last = join(w, w_came, last)
            w_came = swap(w, w_hops.pop(0))
        elif step in ("a", "b"):
            near = last = join(*blocks[step], last)
            blocks[step] = near, swap(near, hops[step].pop(0))
            if not hops[step]:
                latents.append(spread(*blocks[step]))
        elif step == "touch":
            last = touch(w_came, last, step)
        elif step in ("T", "U"):
            last = touch(last, last, step)
        elif step == "take":
            w0 = last = take(wo.T, last)
            wo_came = swap(w0, "h")
        elif step == "o":
            w0 = last = join(w0, wo_came, last)
            w1 = swap(w0, "rs")
            weights = (w0, w1, swap(w0, "sr"), swap(w1, "sr"))
        elif kind == "A":
            out = attention(place, (LATENT_PATHS[s], WEIGHT_PATH), latents[s], (w, w_came), last)
            own.append(out)
            other.append([swap(half, "c") for half in out])
            last = out[1]
        else:
            g = int(step[2])
            path = SUM_PATHS[g]
            if kind == "P":
                send, last = project(place, path, own[s], other[s], weights[g], last)
                sums[s, g] = last, swap(send, path[0])
            elif kind == "+" and g % 2 == 0:
                sums[s, g] = add(*sums[s, g], last)
                last = sums[s, g][0]
            elif kind == "+":
                last, send = add_pair(*sums[s, g - 1], *sums[s, g], last)
                sums[s, g - 1] = last, swap(send, path[1])
            else:
                last, *sends = add_second(*sums[s, g], kept[g] if s else [], last)
                stays[s, g] = last
                if s == 0:
                    kept[g] = sends
                else:
                    thirds[g] = [swap(send, SUM_PATHS[g + i][2]) for i, send in enumerate(sends)]
    mine, its = {}, {}
    for g in thirds:
        mine[g], last = add_last(place, stays[0, g], stays[1, g], *thirds[g], last)
        its[g] = swap(last, "c")
    return collect(place, *(mine[g] for g in (0, 2)), *(its[g] for g in (0, 2)))


def solution(mesh):
    parts = Mesh(mesh.devices.reshape(SIZES), AX)
    dp, tensor = AX[:3], AX[3:]
    in_specs = (
        P(AX, None),
        P(AX, None),
        P(),
        P(),
        P(dp, tensor),
        P(dp, tensor),
        P(tensor, dp),
    )
    return jax.shard_map(
        shards, mesh=parts, in_specs=in_specs, out_specs=P(AX, None), check_vma=False
    )
```

```python
import functools

import jax
import jax.numpy as jnp
import numpy as np
from jax import lax
from jax.experimental import pallas as pl
from jax.experimental.pallas import tpu as pltpu
from jax.sharding import Mesh, PartitionSpec as P

NOPE = 128
R = 64
V = 128
QL = 1536
KL = 512
SEQ = 1024
BLK = 128
EPS = 1e-06
LAT = QL + KL + 2 * R
QW = 4 * (NOPE + R)
KW = 4 * (NOPE + V)
GW = 896
AX = ("y", "xh", "core", "z", "xl")
SIZES = (4, 2, 2, 4, 2)
PIECE = 288
BF = jnp.bfloat16
F32 = jnp.float32


def rope_tables():
    half = R // 2
    freq = 10000.0 ** (-np.arange(half) / half)
    ang = np.arange(SEQ)[:, None] * freq[None, :]
    cos = np.tile(np.cos(ang), (1, 4)).astype(np.float32)
    sin = np.sin(ang)
    sin = np.concatenate([-sin, sin, -sin, sin], axis=1).astype(np.float32)
    return cos, sin


COS, SIN = rope_tables()


def pairs_of(partner):
    out = []
    for source in range(int(np.prod(SIZES))):
        place = np.unravel_index(source, SIZES)
        out.append((source, int(np.ravel_multi_index(partner(*map(int, place)), SIZES))))
    return out


MOVES = {
    "x": lambda y, xh, c, z, xl: (y, xh, c, z, 1 - xl),
    "p": lambda y, xh, c, z, xl: (y, xh, c, z ^ 1, xl),
    "q": lambda y, xh, c, z, xl: (y, xh, c, z ^ 3, xl),
    "h": lambda y, xh, c, z, xl: (y, 1 - xh, c, z, xl),
    "r": lambda y, xh, c, z, xl: (y ^ 1, xh, c, z, xl),
    "s": lambda y, xh, c, z, xl: (y ^ 3, xh, c, z, xl),
    "c": lambda y, xh, c, z, xl: (y, xh, 1 - c, z, xl),
}
RING = {"x": 0, "h": 0, "p": 1, "r": 1, "q": 3, "s": 3}
PAIR = {"x": 1, "h": 1, "p": 0, "r": 0, "q": 0, "s": 0}


@functools.cache
def swap_pairs(moves):
    return pairs_of(lambda *at: MOVES[moves[0] if at[2] == 0 else moves[-1]](*at))


def swap(x, which):
    return lax.ppermute(x, AX, swap_pairs(which))


def steps_of(path, core):
    def choose(a, b):
        return a if a == b else jnp.where(core == 0, a, b)

    return [
        (choose(RING[m[0]], RING[m[-1]]), choose(PAIR[m[0]], PAIR[m[-1]])) for m in path
    ]


def corners(steps):
    out = [(0, 0)]
    for ring, pair in steps:
        out = [(r ^ dr, x ^ dx) for r, x in out for dr, dx in ((0, 0), (ring, pair))]
    return out


def lanes(shape):
    return lax.broadcasted_iota(jnp.int32, shape, len(shape) - 1)


def turn(x):
    return pltpu.roll(x, 64, x.ndim - 1)


def rope_pairs(x, cos, sin):
    low = (lanes(x.shape) // 32) % 2 == 0
    swapped = jnp.where(low, pltpu.roll(x, 96, 1), pltpu.roll(x, 32, 1))
    return x * cos + swapped * sin


ANYWHERE = pl.BlockSpec(memory_space=pl.ANY)
FAR = pl.BlockSpec(memory_space=pltpu.HBM)
PLACE = pl.BlockSpec(memory_space=pltpu.SMEM)
LOCAL = pl.BlockSpec(memory_space=pltpu.VMEM)
WIDE = 60 * 2**20


def cost(name):
    return pl.CostEstimate(
        flops=int(COSTS.get(name, 1) * 10**9), bytes_accessed=2**20, transcendentals=0
    )


def copied(pairs, sems):
    copies = [pltpu.make_async_copy(a, b, sems.at[i]) for i, (a, b) in enumerate(pairs)]
    for copy in copies:
        copy.start()
    return copies


def cut_kernel(place, wk_hbm, wq_hbm, mine, theirs, wk, wq, sems):
    core = place[2]
    for copy in copied(((wk_hbm, wk), (wq_hbm, wq)), sems):
        copy.wait()
    for which, ref in ((1 - core, theirs), (core, mine)):
        at = pl.multiple_of(which * QW, QW)
        ref[:96] = wq[:, pl.ds(at, QW)]
        at = pl.multiple_of(which * KW, KW)
        ref[96:128] = wk[:, pl.ds(at, QW)]
        at = pl.multiple_of(which * KW + QW, KW - QW)
        rest = wk[:, pl.ds(at, KW - QW)]
        ref[128:160] = jnp.concatenate([rest, jnp.zeros((32, 512), BF)], axis=1)


def cut(place, wk, wq):
    out = jax.ShapeDtypeStruct((160, QW), BF)
    return pl.pallas_call(
        cut_kernel,
        out_shape=(out, out),
        in_specs=[PLACE] + [FAR] * 2,
        scratch_shapes=[
            pltpu.VMEM(wk.shape, BF),
            pltpu.VMEM(wq.shape, BF),
            pltpu.SemaphoreType.DMA((2,)),
        ],
        compiler_params=pltpu.CompilerParams(vmem_limit_bytes=WIDE),
        cost_estimate=cost("cut"),
        name="cut",
    )(place, wk, wq)


def pair_kernel(place, mine, came, after, out):
    core = place[2]
    for which, ref in ((core, mine), (1 - core, came)):
        out[pl.ds(pl.multiple_of(which * 96, 96), 96)] = ref[:96]
        out[pl.ds(pl.multiple_of(192 + which * 32, 32), 32)] = ref[96:128]
        at = pl.multiple_of(which * 256, 256)
        out[256:288, pl.ds(at, 256)] = ref[128:160, :256]
    out[256:288, 512:] = jnp.zeros((32, 256), BF)


def pair(place, mine, came, after):
    return pl.pallas_call(
        pair_kernel,
        out_shape=jax.ShapeDtypeStruct((PIECE, QW), BF),
        in_specs=[PLACE, LOCAL, LOCAL, ANYWHERE],
        compiler_params=pltpu.CompilerParams(vmem_limit_bytes=16 * 2**20),
        cost_estimate=cost("pair"),
        name="pair",
    )(place, mine, came, after)


def sort_kernel(place, mine, came, after, first, second):
    zero = place[2] == 0
    first[...] = jnp.where(zero, mine[...], came[...])
    second[...] = jnp.where(zero, came[...], mine[...])


def sort(place, mine, came, after):
    return pl.pallas_call(
        sort_kernel,
        out_shape=(jax.ShapeDtypeStruct(mine.shape, BF),) * 2,
        in_specs=[PLACE, LOCAL, LOCAL, ANYWHERE],
        compiler_params=pltpu.CompilerParams(vmem_limit_bytes=16 * 2**20),
        cost_estimate=cost("sort"),
        name="sort",
    )(place, mine, came, after)


def take_kernel(x, after, out):
    out[...] = x[...]


def take(x, after):
    return pl.pallas_call(
        take_kernel,
        out_shape=jax.ShapeDtypeStruct(x.shape, BF),
        in_specs=[LOCAL, ANYWHERE],
        compiler_params=pltpu.CompilerParams(vmem_limit_bytes=16 * 2**20),
        cost_estimate=cost("take"),
        name="take",
    )(x, after)


def join_kernel(a, b, after, out):
    out[: a.shape[0]] = a[...]
    out[a.shape[0] :] = b[...]


def join(a, b, after):
    return pl.pallas_call(
        join_kernel,
        out_shape=jax.ShapeDtypeStruct((2 * a.shape[0], a.shape[1]), BF),
        in_specs=[LOCAL, LOCAL, ANYWHERE],
        compiler_params=pltpu.CompilerParams(vmem_limit_bytes=16 * 2**20),
        cost_estimate=cost("join"),
        name="join",
    )(a, b, after)


def touch_kernel(x, after, out):
    out[...] = jnp.zeros_like(out)


def touch(x, after, name):
    return pl.pallas_call(
        touch_kernel,
        out_shape=jax.ShapeDtypeStruct((16, 128), BF),
        in_specs=[ANYWHERE, ANYWHERE],
        cost_estimate=cost(name),
        name="touch",
    )(x, after)


def norm_kernel(
    place, q_hbm, kv_hbm, qg_hbm, kvg_hbm, cos_hbm, sin_hbm, after, mine_ref, theirs_ref,
    rows, q_ref, kv_ref, qg_ref, kvg_ref, cos_ref, sin_ref, sems,
):
    core = place[2]
    at = pl.ds(pl.multiple_of((place[3] * 2 + place[4]) * BLK, BLK), BLK)
    copies = copied(
        (
            (q_hbm, q_ref),
            (kv_hbm, kv_ref),
            (qg_hbm, qg_ref),
            (kvg_hbm, kvg_ref),
            (cos_hbm.at[at], cos_ref),
            (sin_hbm.at[at], sin_ref),
        ),
        sems,
    )
    for copy in copies:
        copy.wait()

    def norm(x, gain):
        return x * lax.rsqrt(jnp.mean(x * x, axis=-1, keepdims=True) + EPS) * gain

    kv = kv_ref[...].astype(F32).T
    rows[:, :QL] = norm(q_ref[...].astype(F32), qg_ref[...][None, :]).astype(BF)
    rows[:, QL : QL + KL] = norm(kv[:, :KL], kvg_ref[...][None, :]).astype(BF)
    rot = kv[:, KL:]
    rot = rope_pairs(jnp.concatenate([rot, rot], axis=1), cos_ref[...], sin_ref[...])
    rows[:, QL + KL :] = rot.astype(BF)
    mine_ref[...] = rows[pl.ds(pl.multiple_of(core * 64, 64), 64), :]
    theirs_ref[...] = rows[pl.ds(pl.multiple_of((1 - core) * 64, 64), 64), :]


def norms(place, q_latent, kv_compressed, q_gain, kv_gain, after):
    half = jax.ShapeDtypeStruct((64, LAT), BF)
    return pl.pallas_call(
        norm_kernel,
        out_shape=(half, half),
        in_specs=[PLACE] + [FAR] * 6 + [ANYWHERE],
        scratch_shapes=[
            pltpu.VMEM((BLK, LAT), BF),
            pltpu.VMEM((BLK, QL), BF),
            pltpu.VMEM((KL + R, BLK), BF),
            pltpu.VMEM((QL,), F32),
            pltpu.VMEM((KL,), F32),
            pltpu.VMEM((BLK, 128), F32),
            pltpu.VMEM((BLK, 128), F32),
            pltpu.SemaphoreType.DMA((6,)),
        ],
        compiler_params=pltpu.CompilerParams(vmem_limit_bytes=WIDE),
        cost_estimate=cost("norms"),
        name="norms",
    )(place, q_latent, kv_compressed.T, q_gain, kv_gain, COS, SIN, after)


def attention_kernel(
    paths, place, m0, m1, t0, *refs
):
    t1, refs = refs[:PIECES], refs[PIECES:]
    w0, w1, after, cos_hbm, sin_hbm, o0_ref, o1_ref = refs[:7]
    x, wq, wk, cos_ref, sin_ref, q, kv, sems = refs[7:]
    y, xh, core, z, xl = (place[i] for i in range(5))
    copies = {"x": [], "wk": [], "wq": []}
    count = 0

    def start(kind, source, target):
        nonlocal count
        copy = pltpu.make_async_copy(source, target, sems.at[count])
        copy.start()
        copies[kind].append(copy)
        count += 1

    def blocks(path, owner, near, far):
        first, second, third = steps_of(path, owner)
        for i, (ring, pair) in enumerate(corners((second, first))):
            yield near, i, ring, pair
            yield far, i, ring ^ third[0], pair ^ third[1]

    for half, near, far in ((core, m0, m1), (1 - core, t0, t1)):
        for part, i, zr, xr in blocks(paths[0], half, near, far):
            if isinstance(part, tuple):
                size = 4 // PIECES
                part, i = part[i // size], i % size
            at = ((z ^ zr) * 2 + (xl ^ xr)) * BLK + half * 64
            start("x", part.at[pl.ds(i * 64, 64)], x.at[pl.ds(pl.multiple_of(at, 64), 64)])
    for part, i, yr, xr in blocks(paths[1], core, w0, w1):
        at = (y ^ yr) * 2 + (xh ^ xr)
        rows = pl.ds(pl.multiple_of(at * 64, 64), 64)
        start("wk", part.at[pl.ds(i * PIECE + 192, 64)], wk.at[rows, pl.ds(0, QW)])
        for c in range(2):
            start(
                "wk",
                part.at[pl.ds(i * PIECE + 256, 32), pl.ds(c * 256, 256)],
                wk.at[pl.ds(pl.multiple_of(at * 64 + c * 32, 32), 32), pl.ds(QW, 256)],
            )
    for part, i, yr, xr in blocks(paths[1], core, w0, w1):
        at = (y ^ yr) * 2 + (xh ^ xr)
        rows = pl.ds(pl.multiple_of(at * 192, 192), 192)
        start("wq", part.at[pl.ds(i * PIECE, 192)], wq.at[rows])
    start("wq", cos_hbm, cos_ref)
    start("wq", sin_hbm, sin_ref)
    for copy in copies["x"] + copies["wk"]:
        copy.wait()
    for rows in (pl.ds(0, 512), pl.ds(512, 512)):
        kv[rows, :] = jnp.dot(
            x[rows, QL : QL + KL], wk[...], preferred_element_type=F32
        ).astype(BF)
    for copy in copies["wq"]:
        copy.wait()
    for block in range(4):
        rows = pl.ds(block * 256, 256)
        full = jnp.dot(x[rows, :QL], wq[...], preferred_element_type=F32)
        cos, sin = cos_ref[rows, :], sin_ref[rows, :]
        low = lanes((256, 128)) < 64
        for pair in range(2):
            a, b, c = (full[:, (pair * 3 + i) * 128 : (pair * 3 + i + 1) * 128] for i in range(3))
            rot = rope_pairs(jnp.where(low, b, c), cos, sin).astype(BF)
            other = jnp.where(low, turn(b), turn(c))
            q[rows, pair * 512 : pair * 512 + 128] = a.astype(BF)
            q[rows, pair * 512 + 128 : pair * 512 + 256] = rot
            q[rows, pair * 512 + 256 : pair * 512 + 384] = other.astype(BF)
            q[rows, pair * 512 + 384 : pair * 512 + 512] = rot
    twice = x[:, QL + KL :]
    half_lane = lanes((SEQ, 128)) < 64
    nothing = jnp.zeros_like(twice)
    rots = (jnp.where(half_lane, twice, nothing), jnp.where(half_lane, nothing, twice))
    factor = np.float32(np.log2(np.e) / np.sqrt(NOPE + R))
    causal = lax.broadcasted_iota(jnp.int32, (256, 256), 0) >= lanes((256, 256))
    def scores_of(head, block):
        length = (block + 1) * 256
        rows = slice(block * 256, length)
        return jnp.dot(
            q[rows, head * 256 : (head + 1) * 256],
            keys[head][:, :length],
            preferred_element_type=F32,
        )

    keys = []
    for head in range(4):
        own = jnp.concatenate([kv[:, head * 256 : head * 256 + 128], rots[head % 2]], axis=1)
        keys.append(own.T)
    tasks = [(head, block) for head in range(4) for block in range(4)]
    coming = scores_of(*tasks[0])
    for i, (head, block) in enumerate(tasks):
        scores = coming
        if i + 1 < len(tasks):
            coming = scores_of(*tasks[i + 1])
        length = (block + 1) * 256
        last = jnp.where(causal, scores[:, length - 256 :], -jnp.inf)
        if block:
            scores = jnp.concatenate([scores[:, : length - 256], last], axis=1)
        else:
            scores = last
        highest = jnp.max(scores, axis=1, keepdims=True)
        weight = jnp.exp2((scores - highest) * factor)
        total = jnp.sum(weight, axis=1, keepdims=True)
        out = jnp.dot(
            weight.astype(BF),
            kv[:length, head * 256 + 128 : (head + 1) * 256],
            preferred_element_type=F32,
        )
        column = head % 2 * V
        (o0_ref, o1_ref)[head // 2][block * 256 : length, column : column + V] = (
            out / total
        ).astype(BF)


def attention(place, paths, latents, weights, after):
    return pl.pallas_call(
        functools.partial(attention_kernel, paths),
        out_shape=(jax.ShapeDtypeStruct((SEQ, 2 * V), BF),) * 2,
        in_specs=[PLACE] + [ANYWHERE] * (8 + PIECES),
        scratch_shapes=[
            pltpu.VMEM((SEQ, LAT), BF),
            pltpu.VMEM((QL, QW), BF),
            pltpu.VMEM((KL, KW), BF),
            pltpu.VMEM((SEQ, 128), F32),
            pltpu.VMEM((SEQ, 128), F32),
            pltpu.VMEM((SEQ, 1024), BF),
            pltpu.VMEM((SEQ, KW), BF),
            pltpu.SemaphoreType.DMA((50,)),
        ],
        compiler_params=pltpu.CompilerParams(vmem_limit_bytes=40 * 2**20),
        cost_estimate=cost("attention"),
        name="attention",
    )(place, *latents, *weights, after, COS, SIN)


def project_kernel(path, place, own0, own1, other0, other1, w_hbm, after, send_ref, keep_ref, a, w, sems):
    xh, core, z, xl = (place[i] for i in range(1, 5))
    order = corners(steps_of(path, core))
    order = order[4:] + order[:4]
    pairs = []
    for r in range(2):
        at = pl.multiple_of((xh ^ r) * 448, 448)
        pairs.append((w_hbm.at[pl.ds(r * 448, 448)], w.at[pl.ds(at, 448)]))
    for slot, (zr, xr) in enumerate(order):
        rows = pl.ds(pl.multiple_of(((z ^ zr) * 2 + (xl ^ xr)) * BLK, BLK), BLK)
        for owner, parts in ((core, (own0, own1)), (1 - core, (other0, other1))):
            for i, part in enumerate(parts):
                columns = pl.ds(pl.multiple_of(owner * 512 + i * 256, 256), 256)
                pairs.append((part.at[rows], a.at[pl.ds(slot * BLK, BLK), columns]))
    copies = copied(pairs, sems)
    for half, ref in ((0, send_ref), (1, keep_ref)):
        for copy in copies[half * 18 : half * 16 + 18]:
            copy.wait()
        ref[...] = lax.dot_general(
            a[half * 512 : half * 512 + 512, :],
            w[...],
            (((1,), (1,)), ((), ())),
            preferred_element_type=F32,
        ).astype(BF)


def project(place, path, own, other, weight, after):
    half = jax.ShapeDtypeStruct((512, GW), BF)
    return pl.pallas_call(
        functools.partial(project_kernel, path),
        out_shape=(half, half),
        in_specs=[PLACE] + [ANYWHERE] * 6,
        scratch_shapes=[
            pltpu.VMEM((SEQ, SEQ), BF),
            pltpu.VMEM((GW, SEQ), BF),
            pltpu.SemaphoreType.DMA((34,)),
        ],
        compiler_params=pltpu.CompilerParams(vmem_limit_bytes=24 * 2**20),
        cost_estimate=cost("project"),
        name="project",
    )(place, *own, *other, weight, after)


def total_of(keep, came):
    return (keep.astype(F32) + came.astype(F32)).astype(BF)


def add_kernel(keep, came, after, stay, send):
    total = total_of(keep[...], came[...])
    stay[...] = total[:256]
    send[...] = total[256:]


def add(keep, came, after):
    out = jax.ShapeDtypeStruct((256, GW), BF)
    return pl.pallas_call(
        add_kernel,
        out_shape=(out, out),
        in_specs=[LOCAL, LOCAL, ANYWHERE],
        compiler_params=pltpu.CompilerParams(vmem_limit_bytes=16 * 2**20),
        cost_estimate=cost("add"),
        name="add",
    )(keep, came, after)


def add_pair_kernel(stay0, send0, keep1, came1, after, stay, send):
    total = total_of(keep1[...], came1[...])
    stay[:256] = stay0[...]
    send[:256] = send0[...]
    stay[256:] = total[:256]
    send[256:] = total[256:]


def add_pair(stay0, send0, keep1, came1, after):
    out = jax.ShapeDtypeStruct((512, GW), BF)
    return pl.pallas_call(
        add_pair_kernel,
        out_shape=(out, out),
        in_specs=[LOCAL] * 4 + [ANYWHERE],
        compiler_params=pltpu.CompilerParams(vmem_limit_bytes=24 * 2**20),
        cost_estimate=cost("add_pair"),
        name="add_pair",
    )(stay0, send0, keep1, came1, after)


def add_second_kernel(keep, came, earlier0, earlier1, after, stay, send0, send1):
    for i, (earlier, send) in enumerate(((earlier0, send0), (earlier1, send1))):
        total = total_of(keep[i * 256 : (i + 1) * 256], came[i * 256 : (i + 1) * 256])
        stay[i * BLK : (i + 1) * BLK] = total[:BLK]
        if earlier is None:
            send[...] = total[BLK:]
        else:
            send[:BLK] = earlier[...]
            send[BLK:] = total[BLK:]


def add_second(keep, came, earlier, after):
    rows = BLK * (1 + bool(earlier))
    kernel = add_second_kernel
    if not earlier:
        kernel = lambda keep, came, *refs: add_second_kernel(keep, came, None, None, *refs)
    return pl.pallas_call(
        kernel,
        out_shape=[jax.ShapeDtypeStruct((n, GW), BF) for n in (256, rows, rows)],
        in_specs=[LOCAL] * (2 + len(earlier)) + [ANYWHERE],
        compiler_params=pltpu.CompilerParams(vmem_limit_bytes=24 * 2**20),
        cost_estimate=cost("add_second"),
        name="add_second",
    )(keep, came, *earlier, after)


def add_last_kernel(place, stay0, stay1, came0, came1, after, mine, theirs):
    zero = place[2] == 0
    for i, came in enumerate((came0, came1)):
        rows = slice(i * BLK, (i + 1) * BLK)
        first = total_of(stay0[rows], came[:BLK])
        second = total_of(stay1[rows], came[BLK:])
        mine[rows] = jnp.where(zero, first, second)
        theirs[rows] = jnp.where(zero, second, first)


def add_last(place, stay0, stay1, came0, came1, after):
    out = jax.ShapeDtypeStruct((256, GW), BF)
    return pl.pallas_call(
        add_last_kernel,
        out_shape=(out, out),
        in_specs=[PLACE] + [LOCAL] * 4 + [ANYWHERE],
        compiler_params=pltpu.CompilerParams(vmem_limit_bytes=24 * 2**20),
        cost_estimate=cost("add_last"),
        name="add_last",
    )(place, stay0, stay1, came0, came1, after)


def collect_kernel(place, own0, own1, other0, other1, o_ref):
    own, other = (own0, own1), (other0, other1)
    y, core = place[0], place[2]
    low = lanes((BLK, 128)) < 64
    for g, h, yr in ((0, 0, 0), (1, 2, 1 + 2 * core), (2, 1, 3 - 2 * core), (3, 3, 2)):
        mine = own[g // 2][g % 2 * BLK : (g % 2 + 1) * BLK].astype(F32)
        its = other[h // 2][h % 2 * BLK : (h % 2 + 1) * BLK].astype(F32)
        a, b = jnp.where(core == 0, mine, its), jnp.where(core == 0, its, mine)
        a = [a[:, i * 128 : (i + 1) * 128] for i in range(7)]
        b = [b[:, i * 128 : (i + 1) * 128] for i in range(7)]
        ta, tb = [turn(t) for t in a], [turn(t) for t in b]
        pick = lambda s, t: jnp.where(low, s, t)
        row = a[:3] + [pick(a[3], tb[0])]
        row += [pick(tb[i], tb[i + 1]) for i in range(3)]
        row += [pick(ta[i], ta[i + 1]) for i in range(3, 6)]
        row += [pick(ta[6], b[3])] + b[4:]
        at = pl.multiple_of((y ^ yr) * 2 * GW, 2 * GW)
        o_ref[:, pl.ds(at, 2 * GW)] = jnp.concatenate(row, axis=1).astype(BF)


def collect(place, *parts):
    whole = lambda shape: pl.BlockSpec(shape, lambda i, p: (0, 0))
    return pl.pallas_call(
        collect_kernel,
        out_shape=jax.ShapeDtypeStruct((BLK, 8 * GW), BF),
        grid_spec=pltpu.PrefetchScalarGridSpec(
            num_scalar_prefetch=1,
            grid=(1,),
            in_specs=[whole((2 * BLK, GW))] * 4,
            out_specs=whole((BLK, 8 * GW)),
        ),
        compiler_params=pltpu.CompilerParams(vmem_limit_bytes=24 * 2**20),
        cost_estimate=cost("collect"),
        name="collect",
    )(place, *parts)


LATENT_PATHS = (("xq", "px", "qp"), ("x", "pq", "qp"))
WEIGHT_PATH = ("h", "rs", "sr")
SUM_PATHS = (("xp", "qx", "pq"), ("pq", "qx", "xp"), ("qx", "pq", "xp"), ("xp", "pq", "qx"))
ORDER = (
    *("w", "a", "b", "take", "w", "a", "o", "b", "A0", "P00", "P01", "A1", "+00", "+01",),
    *("P10", "P11", "P12", "P02", "P03", "*00", "P13", "+10", "+11", "+02", "+03", "+12", "+13", "*10",),
    *("*02", "*12",),
)
COSTS = {"project": 4, "attention": 0.1, "take": 2, "join": 6, "add": 0.6, "add_second": 0.3, "add_pair": 1.5, "norms": 1, "cut": 1, "pair": 2}
NORMS_FIRST = False
PIECES = 1


def shards(q_latent, kv_compressed, q_gain, kv_gain, wq_b, wkv_b, wo):
    place = jnp.stack([lax.axis_index(a) for a in AX]).astype(jnp.int32)
    core, xh = place[2], place[1]

    mine_w, theirs_w = cut(place, wkv_b, wq_b)
    came_w = swap(theirs_w, "c")
    if NORMS_FIRST:
        mine, theirs = norms(place, q_latent, kv_compressed, q_gain, kv_gain, mine_w)
        w = last = pair(place, mine_w, came_w, mine)
        came = swap(theirs, "c")
    else:
        w = pair(place, mine_w, came_w, mine_w)
        mine, theirs = norms(place, q_latent, kv_compressed, q_gain, kv_gain, w)
        came = swap(theirs, "c")
        last = mine
    w_came = swap(w, WEIGHT_PATH[0])
    w_hops = list(WEIGHT_PATH[1:])
    a, b = sort(place, mine, came, last)
    last = a
    hops = {"a": list(LATENT_PATHS[0]), "b": list(LATENT_PATHS[1])}
    blocks = {"a": (a, swap(a, hops["a"].pop(0))), "b": (b, swap(b, hops["b"].pop(0)))}

    def spread(near, far):
        size = far.shape[0] // PIECES
        parts = [swap(far[i * size : (i + 1) * size], "c") for i in range(PIECES)]
        return (near, far, swap(near, "c"), *parts)

    latents, own, other, weights = [], [], [], []
    sums, stays, kept, thirds = {}, {}, {}, {}
    for step in ORDER:
        kind, s = step[0], int(step[1]) if step[-1].isdigit() else 0
        if step == "w":
            w = last = join(w, w_came, last)
            w_came = swap(w, w_hops.pop(0))
        elif step in ("a", "b"):
            near = last = join(*blocks[step], last)
            blocks[step] = near, swap(near, hops[step].pop(0))
            if not hops[step]:
                latents.append(spread(*blocks[step]))
        elif step == "touch":
            last = touch(w_came, last, step)
        elif step in ("T", "U"):
            last = touch(last, last, step)
        elif step == "take":
            w0 = last = take(wo.T, last)
            wo_came = swap(w0, "h")
        elif step == "o":
            w0 = last = join(w0, wo_came, last)
            w1 = swap(w0, "rs")
            weights = (w0, w1, swap(w0, "sr"), swap(w1, "sr"))
        elif kind == "A":
            out = attention(place, (LATENT_PATHS[s], WEIGHT_PATH), latents[s], (w, w_came), last)
            own.append(out)
            other.append([swap(half, "c") for half in out])
            last = out[1]
        else:
            g = int(step[2])
            path = SUM_PATHS[g]
            if kind == "P":
                send, last = project(place, path, own[s], other[s], weights[g], last)
                sums[s, g] = last, swap(send, path[0])
            elif kind == "+" and g % 2 == 0:
                sums[s, g] = add(*sums[s, g], last)
                last = sums[s, g][0]
            elif kind == "+":
                last, send = add_pair(*sums[s, g - 1], *sums[s, g], last)
                sums[s, g - 1] = last, swap(send, path[1])
            else:
                last, *sends = add_second(*sums[s, g], kept[g] if s else [], last)
                stays[s, g] = last
                if s == 0:
                    kept[g] = sends
                else:
                    thirds[g] = [swap(send, SUM_PATHS[g + i][2]) for i, send in enumerate(sends)]
    mine, its = {}, {}
    for g in thirds:
        mine[g], last = add_last(place, stays[0, g], stays[1, g], *thirds[g], last)
        its[g] = swap(last, "c")
    return collect(place, *(mine[g] for g in (0, 2)), *(its[g] for g in (0, 2)))


def solution(mesh):
    parts = Mesh(mesh.devices.reshape(SIZES), AX)
    dp, tensor = AX[:3], AX[3:]
    in_specs = (
        P(AX, None),
        P(AX, None),
        P(),
        P(),
        P(dp, tensor),
        P(dp, tensor),
        P(tensor, dp),
    )
    return jax.shard_map(
        shards, mesh=parts, in_specs=in_specs, out_specs=P(AX, None), check_vma=False
    )
```

```python
import functools

import jax
import jax.numpy as jnp
import numpy as np
from jax import lax
from jax.experimental import pallas as pl
from jax.experimental.pallas import tpu as pltpu
from jax.sharding import Mesh, PartitionSpec as P

NOPE = 128
R = 64
V = 128
QL = 1536
KL = 512
SEQ = 1024
BLK = 128
EPS = 1e-06
LAT = QL + KL + 2 * R
QW = 4 * (NOPE + R)
KW = 4 * (NOPE + V)
GW = 896
AX = ("y", "xh", "core", "z", "xl")
SIZES = (4, 2, 2, 4, 2)
PIECE = 288
BF = jnp.bfloat16
F32 = jnp.float32


def rope_tables():
    half = R // 2
    freq = 10000.0 ** (-np.arange(half) / half)
    ang = np.arange(SEQ)[:, None] * freq[None, :]
    cos = np.tile(np.cos(ang), (1, 4)).astype(np.float32)
    sin = np.sin(ang)
    sin = np.concatenate([-sin, sin, -sin, sin], axis=1).astype(np.float32)
    return cos, sin


COS, SIN = rope_tables()


def pairs_of(partner):
    out = []
    for source in range(int(np.prod(SIZES))):
        place = np.unravel_index(source, SIZES)
        out.append((source, int(np.ravel_multi_index(partner(*map(int, place)), SIZES))))
    return out


MOVES = {
    "x": lambda y, xh, c, z, xl: (y, xh, c, z, 1 - xl),
    "p": lambda y, xh, c, z, xl: (y, xh, c, z ^ 1, xl),
    "q": lambda y, xh, c, z, xl: (y, xh, c, z ^ 3, xl),
    "h": lambda y, xh, c, z, xl: (y, 1 - xh, c, z, xl),
    "r": lambda y, xh, c, z, xl: (y ^ 1, xh, c, z, xl),
    "s": lambda y, xh, c, z, xl: (y ^ 3, xh, c, z, xl),
    "c": lambda y, xh, c, z, xl: (y, xh, 1 - c, z, xl),
}
RING = {"x": 0, "h": 0, "p": 1, "r": 1, "q": 3, "s": 3}
PAIR = {"x": 1, "h": 1, "p": 0, "r": 0, "q": 0, "s": 0}


@functools.cache
def swap_pairs(moves):
    return pairs_of(lambda *at: MOVES[moves[0] if at[2] == 0 else moves[-1]](*at))


def swap(x, which):
    return lax.ppermute(x, AX, swap_pairs(which))


def steps_of(path, core):
    def choose(a, b):
        return a if a == b else jnp.where(core == 0, a, b)

    return [
        (choose(RING[m[0]], RING[m[-1]]), choose(PAIR[m[0]], PAIR[m[-1]])) for m in path
    ]


def corners(steps):
    out = [(0, 0)]
    for ring, pair in steps:
        out = [(r ^ dr, x ^ dx) for r, x in out for dr, dx in ((0, 0), (ring, pair))]
    return out


def lanes(shape):
    return lax.broadcasted_iota(jnp.int32, shape, len(shape) - 1)


def turn(x):
    return pltpu.roll(x, 64, x.ndim - 1)


def rope_pairs(x, cos, sin):
    low = (lanes(x.shape) // 32) % 2 == 0
    swapped = jnp.where(low, pltpu.roll(x, 96, 1), pltpu.roll(x, 32, 1))
    return x * cos + swapped * sin


ANYWHERE = pl.BlockSpec(memory_space=pl.ANY)
FAR = pl.BlockSpec(memory_space=pltpu.HBM)
PLACE = pl.BlockSpec(memory_space=pltpu.SMEM)
LOCAL = pl.BlockSpec(memory_space=pltpu.VMEM)
WIDE = 60 * 2**20


def cost(name):
    return pl.CostEstimate(
        flops=int(COSTS.get(name, 1) * 10**9), bytes_accessed=2**20, transcendentals=0
    )


def copied(pairs, sems):
    copies = [pltpu.make_async_copy(a, b, sems.at[i]) for i, (a, b) in enumerate(pairs)]
    for copy in copies:
        copy.start()
    return copies


def cut_kernel(place, wk_hbm, wq_hbm, mine, theirs, wk, wq, sems):
    core = place[2]
    for copy in copied(((wk_hbm, wk), (wq_hbm, wq)), sems):
        copy.wait()
    for which, ref in ((1 - core, theirs), (core, mine)):
        at = pl.multiple_of(which * QW, QW)
        ref[:96] = wq[:, pl.ds(at, QW)]
        at = pl.multiple_of(which * KW, KW)
        ref[96:128] = wk[:, pl.ds(at, QW)]
        at = pl.multiple_of(which * KW + QW, KW - QW)
        rest = wk[:, pl.ds(at, KW - QW)]
        ref[128:160] = jnp.concatenate([rest, jnp.zeros((32, 512), BF)], axis=1)


def cut(place, wk, wq):
    out = jax.ShapeDtypeStruct((160, QW), BF)
    return pl.pallas_call(
        cut_kernel,
        out_shape=(out, out),
        in_specs=[PLACE] + [FAR] * 2,
        scratch_shapes=[
            pltpu.VMEM(wk.shape, BF),
            pltpu.VMEM(wq.shape, BF),
            pltpu.SemaphoreType.DMA((2,)),
        ],
        compiler_params=pltpu.CompilerParams(vmem_limit_bytes=WIDE),
        cost_estimate=cost("cut"),
        name="cut",
    )(place, wk, wq)


def pair_kernel(place, mine, came, after, out):
    core = place[2]
    for which, ref in ((core, mine), (1 - core, came)):
        out[pl.ds(pl.multiple_of(which * 96, 96), 96)] = ref[:96]
        out[pl.ds(pl.multiple_of(192 + which * 32, 32), 32)] = ref[96:128]
        at = pl.multiple_of(which * 256, 256)
        out[256:288, pl.ds(at, 256)] = ref[128:160, :256]
    out[256:288, 512:] = jnp.zeros((32, 256), BF)


def pair(place, mine, came, after):
    return pl.pallas_call(
        pair_kernel,
        out_shape=jax.ShapeDtypeStruct((PIECE, QW), BF),
        in_specs=[PLACE, LOCAL, LOCAL, ANYWHERE],
        compiler_params=pltpu.CompilerParams(vmem_limit_bytes=16 * 2**20),
        cost_estimate=cost("pair"),
        name="pair",
    )(place, mine, came, after)


def sort_kernel(place, mine, came, after, first, second):
    zero = place[2] == 0
    first[...] = jnp.where(zero, mine[...], came[...])
    second[...] = jnp.where(zero, came[...], mine[...])


def sort(place, mine, came, after):
    return pl.pallas_call(
        sort_kernel,
        out_shape=(jax.ShapeDtypeStruct(mine.shape, BF),) * 2,
        in_specs=[PLACE, LOCAL, LOCAL, ANYWHERE],
        compiler_params=pltpu.CompilerParams(vmem_limit_bytes=16 * 2**20),
        cost_estimate=cost("sort"),
        name="sort",
    )(place, mine, came, after)


def take_kernel(x, after, out):
    out[...] = x[...]


def take(x, after):
    return pl.pallas_call(
        take_kernel,
        out_shape=jax.ShapeDtypeStruct(x.shape, BF),
        in_specs=[LOCAL, ANYWHERE],
        compiler_params=pltpu.CompilerParams(vmem_limit_bytes=16 * 2**20),
        cost_estimate=cost("take"),
        name="take",
    )(x, after)


def join_kernel(a, b, after, out):
    out[: a.shape[0]] = a[...]
    out[a.shape[0] :] = b[...]


def join(a, b, after):
    return pl.pallas_call(
        join_kernel,
        out_shape=jax.ShapeDtypeStruct((2 * a.shape[0], a.shape[1]), BF),
        in_specs=[LOCAL, LOCAL, ANYWHERE],
        compiler_params=pltpu.CompilerParams(vmem_limit_bytes=16 * 2**20),
        cost_estimate=cost("join"),
        name="join",
    )(a, b, after)


def touch_kernel(x, after, out):
    out[...] = jnp.zeros_like(out)


def touch(x, after, name):
    return pl.pallas_call(
        touch_kernel,
        out_shape=jax.ShapeDtypeStruct((16, 128), BF),
        in_specs=[ANYWHERE, ANYWHERE],
        cost_estimate=cost(name),
        name="touch",
    )(x, after)


def norm_kernel(
    place, q_hbm, kv_hbm, qg_hbm, kvg_hbm, cos_hbm, sin_hbm, after, mine_ref, theirs_ref,
    rows, q_ref, kv_ref, qg_ref, kvg_ref, cos_ref, sin_ref, sems,
):
    core = place[2]
    at = pl.ds(pl.multiple_of((place[3] * 2 + place[4]) * BLK, BLK), BLK)
    copies = copied(
        (
            (q_hbm, q_ref),
            (kv_hbm, kv_ref),
            (qg_hbm, qg_ref),
            (kvg_hbm, kvg_ref),
            (cos_hbm.at[at], cos_ref),
            (sin_hbm.at[at], sin_ref),
        ),
        sems,
    )
    for copy in copies:
        copy.wait()

    def norm(x, gain):
        return x * lax.rsqrt(jnp.mean(x * x, axis=-1, keepdims=True) + EPS) * gain

    kv = kv_ref[...].astype(F32).T
    rows[:, :QL] = norm(q_ref[...].astype(F32), qg_ref[...][None, :]).astype(BF)
    rows[:, QL : QL + KL] = norm(kv[:, :KL], kvg_ref[...][None, :]).astype(BF)
    rot = kv[:, KL:]
    rot = rope_pairs(jnp.concatenate([rot, rot], axis=1), cos_ref[...], sin_ref[...])
    rows[:, QL + KL :] = rot.astype(BF)
    mine_ref[...] = rows[pl.ds(pl.multiple_of(core * 64, 64), 64), :]
    theirs_ref[...] = rows[pl.ds(pl.multiple_of((1 - core) * 64, 64), 64), :]


def norms(place, q_latent, kv_compressed, q_gain, kv_gain, after):
    half = jax.ShapeDtypeStruct((64, LAT), BF)
    return pl.pallas_call(
        norm_kernel,
        out_shape=(half, half),
        in_specs=[PLACE] + [FAR] * 6 + [ANYWHERE],
        scratch_shapes=[
            pltpu.VMEM((BLK, LAT), BF),
            pltpu.VMEM((BLK, QL), BF),
            pltpu.VMEM((KL + R, BLK), BF),
            pltpu.VMEM((QL,), F32),
            pltpu.VMEM((KL,), F32),
            pltpu.VMEM((BLK, 128), F32),
            pltpu.VMEM((BLK, 128), F32),
            pltpu.SemaphoreType.DMA((6,)),
        ],
        compiler_params=pltpu.CompilerParams(vmem_limit_bytes=WIDE),
        cost_estimate=cost("norms"),
        name="norms",
    )(place, q_latent, kv_compressed.T, q_gain, kv_gain, COS, SIN, after)


def attention_kernel(
    paths, place, m0, m1, t0, *refs
):
    t1, refs = refs[:PIECES], refs[PIECES:]
    w0, w1, after, cos_hbm, sin_hbm, o0_ref, o1_ref = refs[:7]
    x, wq, wk, cos_ref, sin_ref, q, kv, sems = refs[7:]
    y, xh, core, z, xl = (place[i] for i in range(5))
    copies = {"x": [], "wk": [], "wq": []}
    count = 0

    def start(kind, source, target):
        nonlocal count
        copy = pltpu.make_async_copy(source, target, sems.at[count])
        copy.start()
        copies[kind].append(copy)
        count += 1

    def blocks(path, owner, near, far):
        first, second, third = steps_of(path, owner)
        for i, (ring, pair) in enumerate(corners((second, first))):
            yield near, i, ring, pair
            yield far, i, ring ^ third[0], pair ^ third[1]

    for half, near, far in ((core, m0, m1), (1 - core, t0, t1)):
        for part, i, zr, xr in blocks(paths[0], half, near, far):
            if isinstance(part, tuple):
                size = 4 // PIECES
                part, i = part[i // size], i % size
            at = ((z ^ zr) * 2 + (xl ^ xr)) * BLK + half * 64
            start("x", part.at[pl.ds(i * 64, 64)], x.at[pl.ds(pl.multiple_of(at, 64), 64)])
    for part, i, yr, xr in blocks(paths[1], core, w0, w1):
        at = (y ^ yr) * 2 + (xh ^ xr)
        rows = pl.ds(pl.multiple_of(at * 64, 64), 64)
        start("wk", part.at[pl.ds(i * PIECE + 192, 64)], wk.at[rows, pl.ds(0, QW)])
        for c in range(2):
            start(
                "wk",
                part.at[pl.ds(i * PIECE + 256, 32), pl.ds(c * 256, 256)],
                wk.at[pl.ds(pl.multiple_of(at * 64 + c * 32, 32), 32), pl.ds(QW, 256)],
            )
    for part, i, yr, xr in blocks(paths[1], core, w0, w1):
        at = (y ^ yr) * 2 + (xh ^ xr)
        rows = pl.ds(pl.multiple_of(at * 192, 192), 192)
        start("wq", part.at[pl.ds(i * PIECE, 192)], wq.at[rows])
    start("wq", cos_hbm, cos_ref)
    start("wq", sin_hbm, sin_ref)
    for copy in copies["x"] + copies["wk"]:
        copy.wait()
    for rows in (pl.ds(0, 512), pl.ds(512, 512)):
        kv[rows, :] = jnp.dot(
            x[rows, QL : QL + KL], wk[...], preferred_element_type=F32
        ).astype(BF)
    for copy in copies["wq"]:
        copy.wait()
    for block in range(4):
        rows = pl.ds(block * 256, 256)
        full = jnp.dot(x[rows, :QL], wq[...], preferred_element_type=F32)
        cos, sin = cos_ref[rows, :], sin_ref[rows, :]
        low = lanes((256, 128)) < 64
        for pair in range(2):
            a, b, c = (full[:, (pair * 3 + i) * 128 : (pair * 3 + i + 1) * 128] for i in range(3))
            rot = rope_pairs(jnp.where(low, b, c), cos, sin).astype(BF)
            other = jnp.where(low, turn(b), turn(c))
            q[rows, pair * 512 : pair * 512 + 128] = a.astype(BF)
            q[rows, pair * 512 + 128 : pair * 512 + 256] = rot
            q[rows, pair * 512 + 256 : pair * 512 + 384] = other.astype(BF)
            q[rows, pair * 512 + 384 : pair * 512 + 512] = rot
    twice = x[:, QL + KL :]
    half_lane = lanes((SEQ, 128)) < 64
    nothing = jnp.zeros_like(twice)
    rots = (jnp.where(half_lane, twice, nothing), jnp.where(half_lane, nothing, twice))
    factor = np.float32(np.log2(np.e) / np.sqrt(NOPE + R))
    causal = lax.broadcasted_iota(jnp.int32, (256, 256), 0) >= lanes((256, 256))
    def scores_of(head, block):
        length = (block + 1) * 256
        rows = slice(block * 256, length)
        return jnp.dot(
            q[rows, head * 256 : (head + 1) * 256],
            keys[head][:, :length],
            preferred_element_type=F32,
        )

    keys = []
    for head in range(4):
        own = jnp.concatenate([kv[:, head * 256 : head * 256 + 128], rots[head % 2]], axis=1)
        keys.append(own.T)
    tasks = [(head, block) for head in range(4) for block in range(4)]
    coming = scores_of(*tasks[0])
    for i, (head, block) in enumerate(tasks):
        scores = coming
        if i + 1 < len(tasks):
            coming = scores_of(*tasks[i + 1])
        length = (block + 1) * 256
        last = jnp.where(causal, scores[:, length - 256 :], -jnp.inf)
        if block:
            scores = jnp.concatenate([scores[:, : length - 256], last], axis=1)
        else:
            scores = last
        highest = jnp.max(scores, axis=1, keepdims=True)
        weight = jnp.exp2((scores - highest) * factor)
        total = jnp.sum(weight, axis=1, keepdims=True)
        out = jnp.dot(
            weight.astype(BF),
            kv[:length, head * 256 + 128 : (head + 1) * 256],
            preferred_element_type=F32,
        )
        column = head % 2 * V
        (o0_ref, o1_ref)[head // 2][block * 256 : length, column : column + V] = (
            out / total
        ).astype(BF)


def attention(place, paths, latents, weights, after):
    return pl.pallas_call(
        functools.partial(attention_kernel, paths),
        out_shape=(jax.ShapeDtypeStruct((SEQ, 2 * V), BF),) * 2,
        in_specs=[PLACE] + [ANYWHERE] * (8 + PIECES),
        scratch_shapes=[
            pltpu.VMEM((SEQ, LAT), BF),
            pltpu.VMEM((QL, QW), BF),
            pltpu.VMEM((KL, KW), BF),
            pltpu.VMEM((SEQ, 128), F32),
            pltpu.VMEM((SEQ, 128), F32),
            pltpu.VMEM((SEQ, 1024), BF),
            pltpu.VMEM((SEQ, KW), BF),
            pltpu.SemaphoreType.DMA((50,)),
        ],
        compiler_params=pltpu.CompilerParams(vmem_limit_bytes=40 * 2**20),
        cost_estimate=cost("attention"),
        name="attention",
    )(place, *latents, *weights, after, COS, SIN)


def project_kernel(path, place, own0, own1, other0, other1, w_hbm, after, send_ref, keep_ref, a, w, sems):
    xh, core, z, xl = (place[i] for i in range(1, 5))
    order = corners(steps_of(path, core))
    order = order[4:] + order[:4]
    pairs = []
    for r in range(2):
        at = pl.multiple_of((xh ^ r) * 448, 448)
        pairs.append((w_hbm.at[pl.ds(r * 448, 448)], w.at[pl.ds(at, 448)]))
    for slot, (zr, xr) in enumerate(order):
        rows = pl.ds(pl.multiple_of(((z ^ zr) * 2 + (xl ^ xr)) * BLK, BLK), BLK)
        for owner, parts in ((core, (own0, own1)), (1 - core, (other0, other1))):
            for i, part in enumerate(parts):
                columns = pl.ds(pl.multiple_of(owner * 512 + i * 256, 256), 256)
                pairs.append((part.at[rows], a.at[pl.ds(slot * BLK, BLK), columns]))
    copies = copied(pairs, sems)
    for half, ref in ((0, send_ref), (1, keep_ref)):
        for copy in copies[half * 18 : half * 16 + 18]:
            copy.wait()
        ref[...] = lax.dot_general(
            a[half * 512 : half * 512 + 512, :],
            w[...],
            (((1,), (1,)), ((), ())),
            preferred_element_type=F32,
        ).astype(BF)


def project(place, path, own, other, weight, after):
    half = jax.ShapeDtypeStruct((512, GW), BF)
    return pl.pallas_call(
        functools.partial(project_kernel, path),
        out_shape=(half, half),
        in_specs=[PLACE] + [ANYWHERE] * 6,
        scratch_shapes=[
            pltpu.VMEM((SEQ, SEQ), BF),
            pltpu.VMEM((GW, SEQ), BF),
            pltpu.SemaphoreType.DMA((34,)),
        ],
        compiler_params=pltpu.CompilerParams(vmem_limit_bytes=24 * 2**20),
        cost_estimate=cost("project"),
        name="project",
    )(place, *own, *other, weight, after)


def total_of(keep, came):
    return (keep.astype(F32) + came.astype(F32)).astype(BF)


def add_kernel(keep, came, after, stay, send):
    total = total_of(keep[...], came[...])
    stay[...] = total[:256]
    send[...] = total[256:]


def add(keep, came, after):
    out = jax.ShapeDtypeStruct((256, GW), BF)
    return pl.pallas_call(
        add_kernel,
        out_shape=(out, out),
        in_specs=[LOCAL, LOCAL, ANYWHERE],
        compiler_params=pltpu.CompilerParams(vmem_limit_bytes=16 * 2**20),
        cost_estimate=cost("add"),
        name="add",
    )(keep, came, after)


def add_pair_kernel(stay0, send0, keep1, came1, after, stay, send):
    total = total_of(keep1[...], came1[...])
    stay[:256] = stay0[...]
    send[:256] = send0[...]
    stay[256:] = total[:256]
    send[256:] = total[256:]


def add_pair(stay0, send0, keep1, came1, after):
    out = jax.ShapeDtypeStruct((512, GW), BF)
    return pl.pallas_call(
        add_pair_kernel,
        out_shape=(out, out),
        in_specs=[LOCAL] * 4 + [ANYWHERE],
        compiler_params=pltpu.CompilerParams(vmem_limit_bytes=24 * 2**20),
        cost_estimate=cost("add_pair"),
        name="add_pair",
    )(stay0, send0, keep1, came1, after)


def add_second_kernel(keep, came, earlier0, earlier1, after, stay, send0, send1):
    for i, (earlier, send) in enumerate(((earlier0, send0), (earlier1, send1))):
        total = total_of(keep[i * 256 : (i + 1) * 256], came[i * 256 : (i + 1) * 256])
        stay[i * BLK : (i + 1) * BLK] = total[:BLK]
        if earlier is None:
            send[...] = total[BLK:]
        else:
            send[:BLK] = earlier[...]
            send[BLK:] = total[BLK:]


def add_second(keep, came, earlier, after):
    rows = BLK * (1 + bool(earlier))
    kernel = add_second_kernel
    if not earlier:
        kernel = lambda keep, came, *refs: add_second_kernel(keep, came, None, None, *refs)
    return pl.pallas_call(
        kernel,
        out_shape=[jax.ShapeDtypeStruct((n, GW), BF) for n in (256, rows, rows)],
        in_specs=[LOCAL] * (2 + len(earlier)) + [ANYWHERE],
        compiler_params=pltpu.CompilerParams(vmem_limit_bytes=24 * 2**20),
        cost_estimate=cost("add_second"),
        name="add_second",
    )(keep, came, *earlier, after)


def add_last_kernel(place, stay0, stay1, came0, came1, after, mine, theirs):
    zero = place[2] == 0
    for i, came in enumerate((came0, came1)):
        rows = slice(i * BLK, (i + 1) * BLK)
        first = total_of(stay0[rows], came[:BLK])
        second = total_of(stay1[rows], came[BLK:])
        mine[rows] = jnp.where(zero, first, second)
        theirs[rows] = jnp.where(zero, second, first)


def add_last(place, stay0, stay1, came0, came1, after):
    out = jax.ShapeDtypeStruct((256, GW), BF)
    return pl.pallas_call(
        add_last_kernel,
        out_shape=(out, out),
        in_specs=[PLACE] + [LOCAL] * 4 + [ANYWHERE],
        compiler_params=pltpu.CompilerParams(vmem_limit_bytes=24 * 2**20),
        cost_estimate=cost("add_last"),
        name="add_last",
    )(place, stay0, stay1, came0, came1, after)


def collect_kernel(place, own0, own1, other0, other1, o_ref):
    own, other = (own0, own1), (other0, other1)
    y, core = place[0], place[2]
    low = lanes((BLK, 128)) < 64
    for g, h, yr in ((0, 0, 0), (1, 2, 1 + 2 * core), (2, 1, 3 - 2 * core), (3, 3, 2)):
        mine = own[g // 2][g % 2 * BLK : (g % 2 + 1) * BLK].astype(F32)
        its = other[h // 2][h % 2 * BLK : (h % 2 + 1) * BLK].astype(F32)
        a, b = jnp.where(core == 0, mine, its), jnp.where(core == 0, its, mine)
        a = [a[:, i * 128 : (i + 1) * 128] for i in range(7)]
        b = [b[:, i * 128 : (i + 1) * 128] for i in range(7)]
        ta, tb = [turn(t) for t in a], [turn(t) for t in b]
        pick = lambda s, t: jnp.where(low, s, t)
        row = a[:3] + [pick(a[3], tb[0])]
        row += [pick(tb[i], tb[i + 1]) for i in range(3)]
        row += [pick(ta[i], ta[i + 1]) for i in range(3, 6)]
        row += [pick(ta[6], b[3])] + b[4:]
        at = pl.multiple_of((y ^ yr) * 2 * GW, 2 * GW)
        o_ref[:, pl.ds(at, 2 * GW)] = jnp.concatenate(row, axis=1).astype(BF)


def collect(place, *parts):
    whole = lambda shape: pl.BlockSpec(shape, lambda i, p: (0, 0))
    return pl.pallas_call(
        collect_kernel,
        out_shape=jax.ShapeDtypeStruct((BLK, 8 * GW), BF),
        grid_spec=pltpu.PrefetchScalarGridSpec(
            num_scalar_prefetch=1,
            grid=(1,),
            in_specs=[whole((2 * BLK, GW))] * 4,
            out_specs=whole((BLK, 8 * GW)),
        ),
        compiler_params=pltpu.CompilerParams(vmem_limit_bytes=24 * 2**20),
        cost_estimate=cost("collect"),
        name="collect",
    )(place, *parts)


LATENT_PATHS = (("xq", "px", "qp"), ("x", "pq", "qp"))
WEIGHT_PATH = ("h", "rs", "sr")
SUM_PATHS = (("xp", "qx", "pq"), ("pq", "qx", "xp"), ("qx", "pq", "xp"), ("xp", "pq", "qx"))
ORDER = (
    *("w", "a", "b", "take", "w", "a", "o", "b", "A0", "P00", "P01", "A1", "+00", "+01",),
    *("P10", "P11", "P02", "P03", "P12", "P13", "*00", "+10", "+11", "+02", "+03", "+12", "+13", "*10",),
    *("*02", "*12",),
)
COSTS = {"project": 2, "attention": 0.6, "take": 2, "join": 6, "add": 0.6, "add_second": 0.3, "add_pair": 1.5, "norms": 1}
NORMS_FIRST = False
PIECES = 1


def shards(q_latent, kv_compressed, q_gain, kv_gain, wq_b, wkv_b, wo):
    place = jnp.stack([lax.axis_index(a) for a in AX]).astype(jnp.int32)
    core, xh = place[2], place[1]

    mine_w, theirs_w = cut(place, wkv_b, wq_b)
    came_w = swap(theirs_w, "c")
    if NORMS_FIRST:
        mine, theirs = norms(place, q_latent, kv_compressed, q_gain, kv_gain, mine_w)
        w = last = pair(place, mine_w, came_w, mine)
        came = swap(theirs, "c")
    else:
        w = pair(place, mine_w, came_w, mine_w)
        mine, theirs = norms(place, q_latent, kv_compressed, q_gain, kv_gain, w)
        came = swap(theirs, "c")
        last = mine
    w_came = swap(w, WEIGHT_PATH[0])
    w_hops = list(WEIGHT_PATH[1:])
    a, b = sort(place, mine, came, last)
    last = a
    hops = {"a": list(LATENT_PATHS[0]), "b": list(LATENT_PATHS[1])}
    blocks = {"a": (a, swap(a, hops["a"].pop(0))), "b": (b, swap(b, hops["b"].pop(0)))}

    def spread(near, far):
        size = far.shape[0] // PIECES
        parts = [swap(far[i * size : (i + 1) * size], "c") for i in range(PIECES)]
        return (near, far, swap(near, "c"), *parts)

    latents, own, other, weights = [], [], [], []
    sums, stays, kept, thirds = {}, {}, {}, {}
    for step in ORDER:
        kind, s = step[0], int(step[1]) if step[-1].isdigit() else 0
        if step == "w":
            w = last = join(w, w_came, last)
            w_came = swap(w, w_hops.pop(0))
        elif step in ("a", "b"):
            near = last = join(*blocks[step], last)
            blocks[step] = near, swap(near, hops[step].pop(0))
            if not hops[step]:
                latents.append(spread(*blocks[step]))
        elif step == "touch":
            last = touch(w_came, last, step)
        elif step in ("T", "U"):
            last = touch(last, last, step)
        elif step == "take":
            w0 = last = take(wo.T, last)
            wo_came = swap(w0, "h")
        elif step == "o":
            w0 = last = join(w0, wo_came, last)
            w1 = swap(w0, "rs")
            weights = (w0, w1, swap(w0, "sr"), swap(w1, "sr"))
        elif kind == "A":
            out = attention(place, (LATENT_PATHS[s], WEIGHT_PATH), latents[s], (w, w_came), last)
            own.append(out)
            other.append([swap(half, "c") for half in out])
            last = out[1]
        else:
            g = int(step[2])
            path = SUM_PATHS[g]
            if kind == "P":
                send, last = project(place, path, own[s], other[s], weights[g], last)
                sums[s, g] = last, swap(send, path[0])
            elif kind == "+" and g % 2 == 0:
                sums[s, g] = add(*sums[s, g], last)
                last = sums[s, g][0]
            elif kind == "+":
                last, send = add_pair(*sums[s, g - 1], *sums[s, g], last)
                sums[s, g - 1] = last, swap(send, path[1])
            else:
                last, *sends = add_second(*sums[s, g], kept[g] if s else [], last)
                stays[s, g] = last
                if s == 0:
                    kept[g] = sends
                else:
                    thirds[g] = [swap(send, SUM_PATHS[g + i][2]) for i, send in enumerate(sends)]
    mine, its = {}, {}
    for g in thirds:
        mine[g], last = add_last(place, stays[0, g], stays[1, g], *thirds[g], last)
        its[g] = swap(last, "c")
    return collect(place, *(mine[g] for g in (0, 2)), *(its[g] for g in (0, 2)))


def solution(mesh):
    parts = Mesh(mesh.devices.reshape(SIZES), AX)
    dp, tensor = AX[:3], AX[3:]
    in_specs = (
        P(AX, None),
        P(AX, None),
        P(),
        P(),
        P(dp, tensor),
        P(dp, tensor),
        P(tensor, dp),
    )
    return jax.shard_map(
        shards, mesh=parts, in_specs=in_specs, out_specs=P(AX, None), check_vma=False
    )
```
